32 devices in a mesh: pole: 4 (over x, core), row: 2 (over y), col: 4 (over z).
Axes of the slice: x: 2, y: 2, z: 4, core: 2. Of those that a mesh axis runs over, the one named last changes fastest.
Arguments:
- inverse: bfloat16 [12, 2, 6144, 6144], P('pole', None, 'col', 'row'), may hold values from -0.078125 to 0.078125
- lower: bfloat16 [12, 2, 6144, 512], P('pole', None, 'row', 'col'), may hold values from -6 to 6
- mask_tiles: int32 [16, 16], replicated, may hold values from 0 to 1, as said below
- pole_weight: float32 [12, 2], P('pole'), may hold values from -4 to 4
Outputs:
- panel: bfloat16 [12, 2, 6144, 512], P('pole', None, 'col', 'row')
- density: float32 [6144, 512], P(('col', 'pole'), 'row')
The draws below stay inside these ranges and needn't reach their ends.
Inputs may be any that keep to these rules, and one draw needn't show every extreme that they name: `mask_tiles`: each tile row is either all ones or holds exactly one 1; of tile rows t and t + 8 exactly one is all ones.
All inputs are finite; a program needn't handle non-finite values.
Results may differ from the reference program's by a relative error of at most 0.017.
Values may be sent and summed in bfloat16 or wider, within the bound.
No kernel may reach another device: no remote copies, remote signals or barrier semaphores. Data moves between devices by JAX's collectives and lax.ppermute only.
A program may use at most 256 MiB of HBM per device.

```python
import jax
import jax.numpy as jnp
from jax import lax

TILE = 384
NT = 16
PANEL = 512
ORDER = 6144
POLES = 12
N_ROW = 2


def draw_mask_tiles(key, part):
    first_key = jax.random.fold_in(key, 11)
    second_key = jax.random.fold_in(key, 23)
    half_rows = NT // 2
    heavy_low = jax.random.randint(first_key, (half_rows,), 0, 2)
    single_col = jax.random.randint(second_key, (NT,), 0, NT)
    tile_rows = jnp.arange(NT, dtype=jnp.int32)
    tile_cols = jnp.arange(NT, dtype=jnp.int32)
    paired = heavy_low[tile_rows % half_rows]
    heavy = jnp.where(tile_rows < half_rows, paired == 1, paired == 0)
    single = (tile_cols[None, :] == single_col[:, None]).astype(jnp.int32)
    return jnp.where(heavy[:, None], jnp.ones((NT, NT), jnp.int32), single).astype(jnp.int32)


def strengthened(entries, rng, source, target, shards_of, factor):
    def block_of(axis_at):
        return (jnp.arange(entries.shape[axis_at]) // (entries.shape[axis_at] // shards_of)).reshape((-1,) + (1,) * (entries.ndim - 1 - axis_at))

    near = jax.random.permutation(rng, shards_of)[block_of(target)]
    second = (block_of(target) + shards_of // 2) % shards_of
    return jnp.where((block_of(source) == near) | (block_of(source) == second), factor * entries, entries)


def block_scale(stream_key, dims, pieces, least, largest):
    loudness, own = 1.0, jax.random.fold_in(stream_key, 6)
    for axis_at, blocks in pieces:
        heights = jnp.exp(jax.random.uniform(jax.random.fold_in(own, axis_at), (blocks,), jnp.float32, least / len(pieces), largest / len(pieces)))
        loudness = loudness * jnp.repeat(heights, dims[axis_at] // blocks).reshape([-1 if axis == axis_at else 1 for axis in range(len(dims))])
    return loudness


def normal_values(stream_key, shape, deviation, bound, pieces=(), held_as=jnp.bfloat16):
    array = jax.random.normal(stream_key, shape, jnp.float32) * deviation
    if len(pieces) > 0:
        array = block_scale(stream_key, shape, pieces, -0.22, 0.18) * array
    return jnp.clip(array, min=-bound, max=bound).astype(held_as)


def heavy_noise(own_key, dims, deviation, limit, cuts, heavy, kind=jnp.bfloat16):
    array = deviation * jax.random.normal(own_key, dims, jnp.float32)
    if cuts:
        array = array * block_scale(own_key, dims, cuts, -0.22, 0.18)
    return jnp.clip(strengthened(array, jax.random.fold_in(own_key, 3), *heavy), -limit, limit).astype(kind)


def setup_inputs(seed: int = 0) -> dict:
    streams_of = jax.random.split(jax.random.key(seed), 5)
    inverse = normal_values(streams_of[0], (POLES, 2, ORDER, ORDER), ORDER ** -0.5, 0.078125, ((0, 4), (2, 4), (3, 2)))
    lower = heavy_noise(streams_of[1], (POLES, 2, ORDER, PANEL), 1.0, 6.0, ((0, 4), (2, 2), (3, 4)), (2, 3, 4, 2.0))
    mask_tiles = draw_mask_tiles(jax.random.fold_in(streams_of[4], 71), 0)
    pole_weight = normal_values(streams_of[3], (POLES, 2), 1.0, 4.0, ((0, 4),), jnp.float32)
    return dict(inverse=inverse, lower=lower, mask_tiles=mask_tiles, pole_weight=pole_weight)


def reference(inverse, lower, mask_tiles, pole_weight):
    keep = jnp.repeat(jnp.repeat(mask_tiles, TILE, axis=0), TILE, axis=1).astype(jnp.bfloat16)
    width = ORDER // N_ROW
    panels = []
    for pole_idx in range(POLES):
        kept = inverse[pole_idx] * keep[None]
        total = jnp.zeros((2, ORDER, PANEL), jnp.float32)
        for block in range(N_ROW):
            lo_col = block * width
            a_re = kept[0, :, lo_col:lo_col + width]
            a_im = kept[1, :, lo_col:lo_col + width]
            l_re = lower[pole_idx, 0, lo_col:lo_col + width]
            l_im = lower[pole_idx, 1, lo_col:lo_col + width]
            real_part = jnp.dot(a_re, l_re, preferred_element_type=jnp.float32) - jnp.dot(a_im, l_im, preferred_element_type=jnp.float32)
            imag_part = jnp.dot(a_re, l_im, preferred_element_type=jnp.float32) + jnp.dot(a_im, l_re, preferred_element_type=jnp.float32)
            rounded = lax.optimization_barrier(jnp.stack([real_part, imag_part]).astype(jnp.bfloat16))
            total = total + rounded.astype(jnp.float32)
        panels.append((-total).astype(jnp.bfloat16))
    panel = jnp.stack(panels)
    values = panel.astype(jnp.float32)
    density = jnp.sum(pole_weight[:, 0, None, None] * values[:, 1] + pole_weight[:, 1, None, None] * values[:, 0], axis=0)
    return panel, density
```

```python
import functools

import jax
import jax.numpy as jnp
import numpy as np
from jax import lax
from jax.experimental import pallas as pl
from jax.experimental.pallas import tpu as pltpu
from jax.sharding import PartitionSpec as P

ANY = pl.BlockSpec(memory_space=pl.ANY)
SMEM = pl.BlockSpec(memory_space=pltpu.SMEM)
LANES = 128
FULL, SINGLE = 2, 1


def complex_product(block, factors):
    real_part = jnp.einsum(
        "prc,pcw->prw", block[:, 0], factors[:, 0], preferred_element_type=jnp.float32
    ) - jnp.einsum("prc,pcw->prw", block[:, 1], factors[:, 1], preferred_element_type=jnp.float32)
    imag_part = jnp.einsum(
        "prc,pcw->prw", block[:, 0], factors[:, 1], preferred_element_type=jnp.float32
    ) + jnp.einsum("prc,pcw->prw", block[:, 1], factors[:, 0], preferred_element_type=jnp.float32)
    return jnp.stack([real_part, imag_part], axis=1)


def general_body(tile, inverse, lower, mask_tiles, pole_weight):
    full_lower = lax.all_gather(lower, "col", axis=3, tiled=True)
    row_tiles = inverse.shape[2] // tile
    col_tiles = inverse.shape[3] // tile
    start = (lax.axis_index("col") * row_tiles, lax.axis_index("row") * col_tiles)
    own = lax.dynamic_slice(mask_tiles, start, (row_tiles, col_tiles))
    keep = jnp.repeat(jnp.repeat(own, tile, axis=0), tile, axis=1).astype(inverse.dtype)
    partial_value = complex_product(inverse * keep[None, None], full_lower)
    summed = lax.psum_scatter(
        partial_value.astype(jnp.bfloat16), "row", scatter_dimension=3, tiled=True
    ).astype(jnp.float32)
    panel = (-summed).astype(jnp.bfloat16)
    values = panel.astype(jnp.float32)
    weighted = jnp.sum(
        pole_weight[:, 0, None, None] * values[:, 1] + pole_weight[:, 1, None, None] * values[:, 0],
        axis=0,
    )
    density = lax.psum_scatter(
        weighted.astype(jnp.bfloat16), "pole", scatter_dimension=0, tiled=True
    ).astype(jnp.float32)
    return (panel, density)


def slice_kernel(cfg, *refs):
    n_cands = len(cfg["cands"])
    refs = list(refs)
    meta, weight, inv = refs[:3]
    cands = refs[3 : 3 + n_cands]
    refs = refs[3 + n_cands :]
    keep = cfg["kind"] == "keep"
    last = cfg["last"]
    pole, tile, row_tiles, n_pole, base = (cfg[k] for k in ("pole", "tile", "row_tiles", "n_pole", "base"))
    if keep:
        recv = refs.pop(0)
        if cfg["aliased"]:
            refs.pop(0)
    out = refs.pop(0)
    dens = [refs.pop(0) for _ in range(n_pole)] if last else []
    abuf, w1, w2, p1, p2, obuf, asem, wsem, osem = refs[:9]
    refs = refs[9:]
    depth = inv.shape[3]
    width = w1.shape[1] // 2
    n_buf = abuf.shape[0]

    def mode(r):
        return meta[r]

    def single(r):
        return meta[row_tiles + r]

    def fetch(r, act):
        slot = lax.rem(r, n_buf)
        rows = pl.ds(pl.multiple_of(r * tile, tile), tile)

        @pl.when(mode(r) == FULL)
        def _():
            for c in range(2):
                act(pltpu.make_async_copy(inv.at[pole, c, rows, :], abuf.at[slot, c], asem.at[slot, c]))

        @pl.when(mode(r) == SINGLE)
        def _():
            cols = pl.ds(pl.multiple_of(single(r) * tile, tile), tile)
            for c in range(2):
                act(
                    pltpu.make_async_copy(
                        inv.at[pole, c, rows, cols], abuf.at[slot, c, :, pl.ds(0, tile)], asem.at[slot, c]
                    )
                )

    def start(copy):
        copy.start()

    def wait(copy):
        copy.wait()

    def lower_copies(ref):
        halves = (pl.ds(0, width), pl.ds(width, width))
        return [
            pltpu.make_async_copy(ref.at[0], w1.at[:, halves[0]], wsem.at[0]),
            pltpu.make_async_copy(ref.at[1], w1.at[:, halves[1]], wsem.at[1]),
            pltpu.make_async_copy(ref.at[1], w2.at[:, halves[0]], wsem.at[2]),
            pltpu.make_async_copy(ref.at[0], w2.at[:, halves[1]], wsem.at[3]),
        ]

    def cand(i):
        return cands[i].at[pole] if cfg["cands"][i] == "own" else cands[i]

    source = meta[base]
    for i in range(n_cands):

        @pl.when(source == i)
        def _(i=i):
            for copy in lower_copies(cand(i)):
                copy.start()

    for r in range(min(n_buf, row_tiles)):
        fetch(r, start)

    if keep:
        rbuf, rsem = refs[:2]
        refs = refs[2:]
        cols = pl.ds(pl.multiple_of(meta[base + 1] * width, width), width)
        recv_copy = pltpu.make_async_copy(recv, rbuf, rsem)
        recv_copy.start()
    if last:
        pbuf, d32, d16, psem, dsem = refs
        others = [
            pltpu.make_async_copy(out.at[q, :, :, cols], pbuf.at[q], psem.at[q]) for q in range(pole)
        ]
        for copy in others:
            copy.start()

    for copy in lower_copies(cand(0)):
        copy.wait()
    if keep:
        recv_copy.wait()
    if last:
        for copy in others:
            copy.wait()

    def out_copy(r):
        rows = pl.ds(pl.multiple_of(r * tile, tile), tile)
        target = out.at[pole, :, rows, cols] if keep else out.at[:, rows, :]
        return pltpu.make_async_copy(obuf.at[:, rows, :], target, osem.at[r])

    def step(r, carry):
        slot = lax.rem(r, n_buf)
        rows = pl.ds(pl.multiple_of(r * tile, tile), tile)
        fetch(r, wait)

        @pl.when(mode(r) == FULL)
        def _():
            p1[...] = jnp.dot(abuf[slot, 0], w1[...], preferred_element_type=jnp.float32)
            p2[...] = jnp.dot(abuf[slot, 1], w2[...], preferred_element_type=jnp.float32)

        @pl.when(mode(r) == SINGLE)
        def _():
            at = pl.ds(pl.multiple_of(single(r) * tile, tile), tile)
            p1[...] = jnp.dot(abuf[slot, 0, :, :tile], w1[at, :], preferred_element_type=jnp.float32)
            p2[...] = jnp.dot(abuf[slot, 1, :, :tile], w2[at, :], preferred_element_type=jnp.float32)

        @pl.when(mode(r) == 0)
        def _():
            p1[...] = jnp.zeros_like(p1)
            p2[...] = jnp.zeros_like(p2)

        if row_tiles > n_buf:

            @pl.when(r + n_buf < row_tiles)
            def _():
                fetch(r + n_buf, start)

        re = p1[:, :width] - p2[:, :width]
        im = p1[:, width:] + p2[:, width:]
        if keep:
            re = -(re + rbuf[0, rows, :].astype(jnp.float32))
            im = -(im + rbuf[1, rows, :].astype(jnp.float32))
        re = re.astype(jnp.bfloat16)
        im = im.astype(jnp.bfloat16)
        obuf[0, rows, :] = re
        obuf[1, rows, :] = im
        out_copy(r).start()
        if last:
            total = weight[pole, 0] * im.astype(jnp.float32) + weight[pole, 1] * re.astype(jnp.float32)
            for q in range(pole):
                total = total + (
                    weight[q, 0] * pbuf[q, 1, rows, :].astype(jnp.float32)
                    + weight[q, 1] * pbuf[q, 0, rows, :].astype(jnp.float32)
                )
            d32[rows, :] = total
            d16[rows, :] = total.astype(jnp.bfloat16)
        return carry

    lax.fori_loop(0, row_tiles, step, 0)

    if last:
        share = d32.shape[0] // n_pole
        mine = meta[2 * row_tiles]
        copies = []
        for d in range(n_pole):
            block = lax.rem(mine + d, n_pole)
            rows = pl.ds(pl.multiple_of(block * share, share), share)
            copies.append(pltpu.make_async_copy((d16 if d else d32).at[rows, :], dens[d], dsem.at[d]))
        for copy in copies:
            copy.start()
        for copy in copies:
            copy.wait()

    def drain(r, carry):
        out_copy(r).wait()
        return carry

    lax.fori_loop(0, row_tiles, drain, 0)


def slice_product(cfg, meta, weight, inverse, cands, recv=None, panel=None):
    poles, _, rows, depth = inverse.shape
    width = cands[0].shape[-1]
    tile, row_tiles, n_pole = cfg["tile"], cfg["row_tiles"], cfg["n_pole"]
    keep, last = cfg["kind"] == "keep", cfg["last"]
    n_buf = min(row_tiles, 4)
    half_shape = (2, rows, width)
    operands = [meta, weight, inverse, *cands]
    specs = [SMEM, SMEM] + [ANY] * (1 + len(cands))
    aliases = {}
    outs = []
    if keep:
        operands.append(recv)
        specs.append(ANY)
        outs.append(jax.ShapeDtypeStruct((poles, 2, rows, cfg["panel_width"]), jnp.bfloat16))
        if panel is not None:
            aliases = {len(operands): 0}
            operands.append(panel)
            specs.append(ANY)
    else:
        outs.append(jax.ShapeDtypeStruct(half_shape, jnp.bfloat16))
    if last:
        share = rows // n_pole
        for d in range(n_pole):
            outs.append(jax.ShapeDtypeStruct((share, width), jnp.bfloat16 if d else jnp.float32))
    scratch = [
        pltpu.VMEM((n_buf, 2, tile, depth), jnp.bfloat16),
        pltpu.VMEM((depth, 2 * width), jnp.bfloat16),
        pltpu.VMEM((depth, 2 * width), jnp.bfloat16),
        pltpu.VMEM((tile, 2 * width), jnp.float32),
        pltpu.VMEM((tile, 2 * width), jnp.float32),
        pltpu.VMEM(half_shape, jnp.bfloat16),
        pltpu.SemaphoreType.DMA((n_buf, 2)),
        pltpu.SemaphoreType.DMA((4,)),
        pltpu.SemaphoreType.DMA((row_tiles,)),
    ]
    if keep:
        scratch += [pltpu.VMEM(half_shape, jnp.bfloat16), pltpu.SemaphoreType.DMA]
    if last:
        scratch += [
            pltpu.VMEM((max(poles - 1, 1), *half_shape), jnp.bfloat16),
            pltpu.VMEM((rows, width), jnp.float32),
            pltpu.VMEM((rows, width), jnp.bfloat16),
            pltpu.SemaphoreType.DMA((max(poles - 1, 1),)),
            pltpu.SemaphoreType.DMA((n_pole,)),
        ]
    cfg = dict(cfg, aliased=panel is not None)
    return pl.pallas_call(
        functools.partial(slice_kernel, cfg),
        out_shape=outs,
        in_specs=specs,
        out_specs=[ANY] * len(outs),
        scratch_shapes=scratch,
        input_output_aliases=aliases,
        compiler_params=pltpu.CompilerParams(vmem_limit_bytes=48 * 2**20),
        cost_estimate=pl.CostEstimate(
            flops=rows * depth, bytes_accessed=rows * width, transcendentals=0
        ),
        name=cfg["name"],
    )(*operands)


def half_order(n_col, half, z):
    group = n_col // 2
    return sorted(range(half * group, (half + 1) * group), key=lambda s: abs(s - z))


def plan_transfers(n_col, poles):
    end = poles - 1
    where = {}

    def forward(name, pole, step, senders, payload):
        senders = [z for z in senders if z <= n_col - step]
        for z in senders:
            for y in range(2):
                where[(z - 1, y, pole, z + step - 1)] = name
        return (name, [(z, z - 1) for z in senders], payload, None)

    slots = []
    for step in range(1, n_col):
        for pole in range(end):
            payload = ("own", pole) if step == 1 else f"p{pole}s{step - 1}"
            slots.append([forward(f"p{pole}s{step}", pole, step, range(1, n_col), payload)])
    slots[2].append(forward(f"p{end}s1", end, 1, range(3, n_col), ("own", end)))
    free = len(slots) - (n_col - 2)
    slots[free].append(forward(f"p{end}s1b", end, 1, [2], ("own", end)))
    for step in range(2, n_col - 1):
        payload = f"p{end}s{step - 1}"
        slots[free + step - 1].append(forward(f"p{end}s{step}", end, step, range(2, n_col), payload))
    natural = list(range(1, n_col))
    turned = sorted(natural, key=lambda s: (s < n_col // 2, s))

    def at_one(s):
        return ("own", end) if s == 1 else f"p{end}s1b" if s == 2 else f"p{end}s{s - 1}"

    for i, (a, b) in enumerate(zip(natural, turned)):
        slots.append([(f"e{i}", [(1, 0)], at_one(a), at_one(b))])
        where[(0, 1, end, a)] = where[(0, 0, end, b)] = f"e{i}"
    return slots, where


def make_fast_body(n_col, n_pole, tile):
    group = n_col // 2

    def body(inverse, lower, mask_tiles, pole_weight):
        poles, _, rows, depth = inverse.shape
        width = lower.shape[3]
        row_tiles, col_tiles = rows // tile, depth // tile
        end = poles - 1
        z, y, mine = lax.axis_index("col"), lax.axis_index("row"), lax.axis_index("pole")
        slots, where_left = plan_transfers(n_col, poles)

        where = {}
        for zz in range(n_col):
            for yy in range(2):
                for p in range(poles):
                    where[(zz, yy, p, zz)] = "own"
                    for s in range(n_col):
                        if s > zz:
                            where[(zz, yy, p, s)] = "L" + where_left[(zz, yy, p, s)]
                        elif s < zz:
                            mirrored = (n_col - 1 - zz, 1 - yy, p, n_col - 1 - s)
                            where[(zz, yy, p, s)] = "R" + where_left[mirrored]
        calls = {}
        tables = []
        for p in range(poles):
            for kind in ("send", "keep"):
                for i in range(group):
                    names, picks = [], np.zeros((n_col, 2), np.int32)
                    columns = np.zeros((n_col, 2), np.int32)
                    for zz in range(n_col):
                        for yy in range(2):
                            half = yy if kind == "keep" else 1 - yy
                            s = half_order(n_col, half, zz)[i]
                            name = where[(zz, yy, p, s)]
                            if name not in names:
                                names.append(name)
                            picks[zz, yy] = names.index(name)
                            columns[zz, yy] = s - half * group
                    calls[(p, kind, i)] = (names, len(tables))
                    tables += [picks, columns]
        chosen = lax.dynamic_slice(jnp.asarray(np.stack(tables)), (0, z, y), (len(tables), 1, 1)).reshape(-1)

        own = lax.dynamic_slice(mask_tiles, (z * row_tiles, y * col_tiles), (row_tiles, col_tiles))
        count = jnp.sum(own, axis=1)
        modes = jnp.where(count == col_tiles, FULL, jnp.where(count == 0, 0, SINGLE))
        single = jnp.argmax(own, axis=1)
        head = jnp.concatenate([modes, single, jnp.reshape(mine, (1,))]).astype(jnp.int32)
        meta = jnp.concatenate([head, chosen])

        arrays = {"own": lower}
        ready = {"own": -1}
        held = {}
        rest = lower
        for p in range(poles):
            held[("own", p)] = rest[p]
            rest, held[("own", p)] = lax.optimization_barrier((rest, held[("own", p)]))

        def operand(prefix, name):
            return held[name] if isinstance(name, tuple) else arrays[prefix + name]

        state = {"panel": None, "sent": {}}
        dens = {}

        def run(p, kind, i):
            names, at = calls[(p, kind, i)]
            cfg = dict(
                name=f"{kind}_{p}_{i}",
                kind=kind,
                last=kind == "keep" and p == end,
                cands=names,
                pole=p,
                tile=tile,
                row_tiles=row_tiles,
                n_pole=n_pole,
                base=head.shape[0] + at,
                panel_width=group * width,
            )
            cands = [arrays[name] for name in names]
            if kind == "send":
                (part,) = slice_product(cfg, meta, pole_weight, inverse, cands)
                state["sent"][(p, i)] = lax.ppermute(part, "row", [(0, 1), (1, 0)])
                return (p, i)
            panel, *shares = slice_product(
                cfg, meta, pole_weight, inverse, cands, state["sent"][(p, i)], state["panel"]
            )
            state["panel"] = panel
            if shares:
                total = shares[0]
                for d in range(1, n_pole):
                    moved = lax.ppermute(
                        shares[d], "pole", [(q, (q + d) % n_pole) for q in range(n_pole)]
                    )
                    total = total + moved.astype(jnp.float32)
                dens[i] = (total, chosen[at + 1])
            return panel

        for t, slot in enumerate(slots):
            for name, _, _, _ in slot:
                ready["L" + name] = ready["R" + name] = t
        queue = [[] for _ in range(len(slots) + 1)]
        final = len(slots) - 1
        for (p, kind, i), (names, _) in calls.items():
            t = max(max(ready[name] for name in names), 0)
            if kind == "keep":
                sent = max(ready[name] for name in calls[(p, "send", i)][0])
                t = max(t, min(sent + 1, final))
            queue[t].append((kind == "keep", p, i))

        done = {}
        computed = {-1: []}

        def launch(t):
            values = []
            for name, pairs, payload, turned in slots[t]:
                for prefix in ("L", "R"):
                    value = operand(prefix, payload)
                    if turned is not None:
                        value = jnp.where(y == (0 if prefix == "L" else 1), operand(prefix, turned), value)
                    values.append(value)
            deps = done.get(t - 2, []) + [state["sent"][key] for key in computed.get(t - 4, [])]
            if state["panel"] is not None:
                values, state["panel"], _ = lax.optimization_barrier((values, state["panel"], deps))
            else:
                values, _ = lax.optimization_barrier((values, deps))
            done[t] = []
            for name, pairs, _, _ in slots[t]:
                for prefix in ("L", "R"):
                    ways = pairs if prefix == "L" else [(n_col - 1 - a, n_col - 1 - b) for a, b in pairs]
                    arrays[prefix + name] = lax.ppermute(values.pop(0), "col", ways)
                    done[t].append(arrays[prefix + name])

        launch(0)
        launch(1)
        for t in range(len(slots)):
            if t + 2 < len(slots):
                launch(t + 2)
            computed[t] = []
            for keep, p, i in sorted(queue[t]):
                out = run(p, "keep" if keep else "send", i)
                if not keep:
                    computed[t].append(out)

        columns = []
        for c in range(group):
            value = dens[0][0]
            for i in range(1, group):
                value = jnp.where(dens[i][1] == c, dens[i][0], value)
            columns.append(value)
        return (state["panel"], jnp.concatenate(columns, axis=1))

    return body


def solution(mesh):
    n_pole, n_row, n_col = (mesh.shape[name] for name in ("pole", "row", "col"))

    def whole(inverse, lower, mask_tiles, pole_weight):
        tile = inverse.shape[2] // mask_tiles.shape[0]
        width = lower.shape[3] // n_col
        rows = inverse.shape[2] // n_col
        fits = n_row == 2 and n_col % 2 == 0 and n_col > 2 and width % LANES == 0
        fits = fits and tile % LANES == 0 and rows % (16 * n_pole) == 0 and inverse.shape[0] > n_pole
        if fits:
            body = make_fast_body(n_col, n_pole, tile)
        else:
            body = functools.partial(general_body, tile)
        return jax.shard_map(
            body,
            mesh=mesh,
            in_specs=(
                P("pole", None, "col", "row"),
                P("pole", None, "row", "col"),
                P(),
                P("pole", None),
            ),
            out_specs=(P("pole", None, "col", "row"), P(("col", "pole"), "row")),
            check_vma=False,
        )(inverse, lower, mask_tiles, pole_weight)

    return whole
```

```python
import functools

import jax
import jax.numpy as jnp
import numpy as np
from jax import lax
from jax.experimental import pallas as pl
from jax.experimental.pallas import tpu as pltpu
from jax.sharding import PartitionSpec as P

ANY = pl.BlockSpec(memory_space=pl.ANY)
SMEM = pl.BlockSpec(memory_space=pltpu.SMEM)
LANES = 128
FULL, SINGLE = 2, 1


def complex_product(block, factors):
    real_part = jnp.einsum(
        "prc,pcw->prw", block[:, 0], factors[:, 0], preferred_element_type=jnp.float32
    ) - jnp.einsum("prc,pcw->prw", block[:, 1], factors[:, 1], preferred_element_type=jnp.float32)
    imag_part = jnp.einsum(
        "prc,pcw->prw", block[:, 0], factors[:, 1], preferred_element_type=jnp.float32
    ) + jnp.einsum("prc,pcw->prw", block[:, 1], factors[:, 0], preferred_element_type=jnp.float32)
    return jnp.stack([real_part, imag_part], axis=1)


def general_body(tile, inverse, lower, mask_tiles, pole_weight):
    full_lower = lax.all_gather(lower, "col", axis=3, tiled=True)
    row_tiles = inverse.shape[2] // tile
    col_tiles = inverse.shape[3] // tile
    start = (lax.axis_index("col") * row_tiles, lax.axis_index("row") * col_tiles)
    own = lax.dynamic_slice(mask_tiles, start, (row_tiles, col_tiles))
    keep = jnp.repeat(jnp.repeat(own, tile, axis=0), tile, axis=1).astype(inverse.dtype)
    partial_value = complex_product(inverse * keep[None, None], full_lower)
    summed = lax.psum_scatter(
        partial_value.astype(jnp.bfloat16), "row", scatter_dimension=3, tiled=True
    ).astype(jnp.float32)
    panel = (-summed).astype(jnp.bfloat16)
    values = panel.astype(jnp.float32)
    weighted = jnp.sum(
        pole_weight[:, 0, None, None] * values[:, 1] + pole_weight[:, 1, None, None] * values[:, 0],
        axis=0,
    )
    density = lax.psum_scatter(
        weighted.astype(jnp.bfloat16), "pole", scatter_dimension=0, tiled=True
    ).astype(jnp.float32)
    return (panel, density)


def slice_kernel(cfg, *refs):
    pole, tile, row_tiles, n_pole = (cfg[k] for k in ("pole", "tile", "row_tiles", "n_pole"))
    parts = cfg["parts"]
    n_parts = len(parts)
    keep, last = cfg["kind"] == "keep", cfg["last"]
    refs = list(refs)

    def take(count):
        taken = refs[:count]
        del refs[:count]
        return taken

    meta, weight, inv = take(3)
    cands = dict(zip(cfg["arrays"], take(len(cfg["arrays"]))))
    if keep:
        recv = take(n_parts)
        take(1 if cfg["aliased"] else 0)
    outs = take(1 if keep else n_parts)
    dens = take(n_pole if last else 0)
    abuf, w1, w2, p1, p2, obuf, asem, wsem, osem = take(9)
    width = w1.shape[1] // (2 * n_parts)
    n_buf = abuf.shape[0]

    def start(copy):
        copy.start()

    def wait(copy):
        copy.wait()

    def tile_rows(r):
        return pl.ds(pl.multiple_of(r * tile, tile), tile)

    def fetch(r, act):
        slot = lax.rem(r, n_buf)

        @pl.when(meta[r] == FULL)
        def _():
            for c in range(2):
                act(pltpu.make_async_copy(inv.at[pole, c, tile_rows(r), :], abuf.at[slot, c], asem.at[slot, c]))

        @pl.when(meta[r] == SINGLE)
        def _():
            cols = tile_rows(meta[row_tiles + r])
            for c in range(2):
                act(
                    pltpu.make_async_copy(
                        inv.at[pole, c, tile_rows(r), cols], abuf.at[slot, c, :, pl.ds(0, tile)], asem.at[slot, c]
                    )
                )

    def lower_copies(j, ref):
        low, high = (pl.ds((2 * j + h) * width, width) for h in range(2))
        return [
            pltpu.make_async_copy(ref.at[0], w1.at[:, low], wsem.at[j, 0]),
            pltpu.make_async_copy(ref.at[1], w1.at[:, high], wsem.at[j, 1]),
            pltpu.make_async_copy(ref.at[1], w2.at[:, low], wsem.at[j, 2]),
            pltpu.make_async_copy(ref.at[0], w2.at[:, high], wsem.at[j, 3]),
        ]

    def source(name):
        return cands[name].at[pole] if name == "own" else cands[name]

    for j, (names, base) in enumerate(parts):
        for i, name in enumerate(names):

            @pl.when(meta[base] == i)
            def _(j=j, name=name):
                for copy in lower_copies(j, source(name)):
                    copy.start()

    for r in range(min(n_buf, row_tiles)):
        fetch(r, start)

    columns = [pl.ds(pl.multiple_of(meta[base + 1] * width, width), width) for _, base in parts]
    if keep:
        rbuf, rsem = take(2)
        recv_copies = [pltpu.make_async_copy(recv[j], rbuf.at[j], rsem.at[j]) for j in range(n_parts)]
        for copy in recv_copies:
            copy.start()
    others = []
    if last:
        pbuf, d32, d16, psem, dsem = take(5)
        others = [
            pltpu.make_async_copy(outs[0].at[q, :, :, columns[0]], pbuf.at[q], psem.at[q]) for q in range(pole)
        ]
        for copy in others:
            copy.start()

    for j, (names, _) in enumerate(parts):
        for copy in lower_copies(j, source(names[0])):
            copy.wait()
    for copy in recv_copies if keep else []:
        copy.wait()
    for copy in others:
        copy.wait()

    def out_copy(r, j):
        rows = tile_rows(r)
        target = outs[0].at[pole, :, rows, columns[j]] if keep else outs[j].at[:, rows, :]
        return pltpu.make_async_copy(obuf.at[j, :, rows, :], target, osem.at[r, j])

    def step(r, carry):
        slot = lax.rem(r, n_buf)
        rows = tile_rows(r)
        fetch(r, wait)

        @pl.when(meta[r] == FULL)
        def _():
            p1[...] = jnp.dot(abuf[slot, 0], w1[...], preferred_element_type=jnp.float32)
            p2[...] = jnp.dot(abuf[slot, 1], w2[...], preferred_element_type=jnp.float32)

        @pl.when(meta[r] == SINGLE)
        def _():
            at = tile_rows(meta[row_tiles + r])
            p1[...] = jnp.dot(abuf[slot, 0, :, :tile], w1[at, :], preferred_element_type=jnp.float32)
            p2[...] = jnp.dot(abuf[slot, 1, :, :tile], w2[at, :], preferred_element_type=jnp.float32)

        @pl.when(meta[r] == 0)
        def _():
            p1[...] = jnp.zeros_like(p1)
            p2[...] = jnp.zeros_like(p2)

        if row_tiles > n_buf:

            @pl.when(r + n_buf < row_tiles)
            def _():
                fetch(r + n_buf, start)

        for j in range(n_parts):
            low, high = (pl.ds((2 * j + h) * width, width) for h in range(2))
            re = p1[:, low] - p2[:, low]
            im = p1[:, high] + p2[:, high]
            if keep:
                re = -(re + rbuf[j, 0, rows, :].astype(jnp.float32))
                im = -(im + rbuf[j, 1, rows, :].astype(jnp.float32))
            re = re.astype(jnp.bfloat16)
            im = im.astype(jnp.bfloat16)
            obuf[j, 0, rows, :] = re
            obuf[j, 1, rows, :] = im
            out_copy(r, j).start()
        if last:
            total = weight[pole, 0] * im.astype(jnp.float32) + weight[pole, 1] * re.astype(jnp.float32)
            for q in range(pole):
                total = total + (
                    weight[q, 0] * pbuf[q, 1, rows, :].astype(jnp.float32)
                    + weight[q, 1] * pbuf[q, 0, rows, :].astype(jnp.float32)
                )
            d32[rows, :] = total
            d16[rows, :] = total.astype(jnp.bfloat16)
        return carry

    lax.fori_loop(0, row_tiles, step, 0)

    if last:
        share = d32.shape[0] // n_pole
        mine = meta[2 * row_tiles]
        copies = []
        for d in range(n_pole):
            block = lax.rem(mine + d, n_pole)
            rows = pl.ds(pl.multiple_of(block * share, share), share)
            copies.append(pltpu.make_async_copy((d16 if d else d32).at[rows, :], dens[d], dsem.at[d]))
        for copy in copies:
            copy.start()
        for copy in copies:
            copy.wait()

    def drain(r, carry):
        for j in range(n_parts):
            out_copy(r, j).wait()
        return carry

    lax.fori_loop(0, row_tiles, drain, 0)


def slice_product(cfg, meta, weight, inverse, arrays, width, recv=None, panel=None):
    poles, _, rows, depth = inverse.shape
    tile, row_tiles, n_pole, parts = cfg["tile"], cfg["row_tiles"], cfg["n_pole"], cfg["parts"]
    keep, last = cfg["kind"] == "keep", cfg["last"]
    n_buf = min(row_tiles, 4)
    n_parts = len(parts)
    names = sorted({name for part, _ in parts for name in part})
    part_shape = (2, rows, width)
    operands = [meta, weight, inverse, *(arrays[name] for name in names)]
    specs = [SMEM, SMEM] + [ANY] * (1 + len(names))
    aliases = {}
    outs = []
    if keep:
        operands += recv
        specs += [ANY] * n_parts
        outs.append(jax.ShapeDtypeStruct((poles, 2, rows, cfg["panel_width"]), jnp.bfloat16))
        if panel is not None:
            aliases = {len(operands): 0}
            operands.append(panel)
            specs.append(ANY)
    else:
        outs += [jax.ShapeDtypeStruct(part_shape, jnp.bfloat16)] * n_parts
    if last:
        share = rows // n_pole
        for d in range(n_pole):
            outs.append(jax.ShapeDtypeStruct((share, width), jnp.bfloat16 if d else jnp.float32))
    scratch = [
        pltpu.VMEM((n_buf, 2, tile, depth), jnp.bfloat16),
        pltpu.VMEM((depth, 2 * width * n_parts), jnp.bfloat16),
        pltpu.VMEM((depth, 2 * width * n_parts), jnp.bfloat16),
        pltpu.VMEM((tile, 2 * width * n_parts), jnp.float32),
        pltpu.VMEM((tile, 2 * width * n_parts), jnp.float32),
        pltpu.VMEM((n_parts, *part_shape), jnp.bfloat16),
        pltpu.SemaphoreType.DMA((n_buf, 2)),
        pltpu.SemaphoreType.DMA((n_parts, 4)),
        pltpu.SemaphoreType.DMA((row_tiles, n_parts)),
    ]
    if keep:
        scratch += [pltpu.VMEM((n_parts, *part_shape), jnp.bfloat16), pltpu.SemaphoreType.DMA((n_parts,))]
    if last:
        scratch += [
            pltpu.VMEM((max(poles - 1, 1), *part_shape), jnp.bfloat16),
            pltpu.VMEM((rows, width), jnp.float32),
            pltpu.VMEM((rows, width), jnp.bfloat16),
            pltpu.SemaphoreType.DMA((max(poles - 1, 1),)),
            pltpu.SemaphoreType.DMA((n_pole,)),
        ]
    cfg = dict(cfg, aliased=panel is not None, arrays=names)
    return pl.pallas_call(
        functools.partial(slice_kernel, cfg),
        out_shape=outs,
        in_specs=specs,
        out_specs=[ANY] * len(outs),
        scratch_shapes=scratch,
        input_output_aliases=aliases,
        compiler_params=pltpu.CompilerParams(vmem_limit_bytes=48 * 2**20),
        cost_estimate=pl.CostEstimate(flops=30 * rows * depth * n_parts, bytes_accessed=rows * width, transcendentals=0),
        name=cfg["name"],
    )(*operands)


def half_order(n_col, half, z):
    group = n_col // 2
    return sorted(range(half * group, (half + 1) * group), key=lambda s: abs(s - z))


def plan_transfers(n_col, poles):
    end, half = poles - 1, n_col // 2
    where = {(z, y, p, z): ("own", p) for z in range(n_col) for y in range(2) for p in range(poles)}
    lists = {"out": [], "across": [], "in": []}
    at = {}

    def add(kind, name, moves):
        moves = [m for m in moves if m[3] < n_col and m[4] < n_col]
        if not moves:
            return
        both = moves + [
            (n_col - 1 - z, n_col - 1 - to, p, n_col - 1 - s1, n_col - 1 - s0) for z, to, p, s0, s1 in moves
        ]
        for z, to, p, s0, s1 in both:
            where[(to, 0, p, s0)] = where[(to, 1, p, s1)] = name
        at[name] = len(lists[kind])
        lists[kind].append((name, both))

    def hop(z, p, step):
        return (z, z - 1, p, z + step - 1, z + step - 1)

    steps = range(1, n_col)
    pairs = [(p, step) for p in range(end) for step in steps]
    for p, step in sorted(pairs, key=lambda item: (item[0] * (n_col - 1) + item[1] - 3 * (item[1] == 1), item)):
        add("out", f"o{p}s{step}", [hop(z, p, step) for z in range(1, half)])
    natural = list(steps)
    turned = sorted(natural, key=lambda s: (s < half, s))
    for i, (a, b) in enumerate(zip(natural, turned)):
        far = [hop(z, end, i + 1) for z in range(2, half)]
        add("out", f"o{end}s{i + 1}", [(1, 0, end, b, a)] + [m for m in far if m[3] < n_col])
    for p in range(poles):
        for step in steps:
            add("across", f"a{p}s{step}", [hop(half, p, step)])
    for p in range(poles):
        for step in steps:
            add("in", f"i{p}s{step}", [hop(z, p, step) for z in range(half + 1, n_col)])
    return lists, where, at


def make_fast_body(n_col, n_pole, tile):
    group = n_col // 2
    places = [(zz, yy) for zz in range(n_col) for yy in range(2)]

    def body(inverse, lower, mask_tiles, pole_weight):
        poles, _, rows, depth = inverse.shape
        width = lower.shape[3]
        row_tiles, col_tiles = rows // tile, depth // tile
        end = poles - 1
        z, y, mine = lax.axis_index("col"), lax.axis_index("row"), lax.axis_index("pole")
        lists, where, ready = plan_transfers(n_col, poles)
        final = len(lists["out"]) - 1

        head_size = 2 * row_tiles + 1
        tables = []
        calls = []
        for p in range(poles):
            whole, single = [list(range(group))], [[i] for i in range(group)]
            for kind in ("send", "keep"):
                for bunch in single if p >= end - 1 else whole:
                    parts = []
                    for i in bunch:
                        names, picks, columns = [], np.zeros((n_col, 2), np.int32), np.zeros((n_col, 2), np.int32)
                        for zz, yy in places:
                            half = yy if kind == "keep" else 1 - yy
                            s = half_order(n_col, half, zz)[i]
                            name = where[(zz, yy, p, s)]
                            name = "own" if isinstance(name, tuple) else name
                            if name not in names:
                                names.append(name)
                            picks[zz, yy] = names.index(name)
                            columns[zz, yy] = s - half * group
                        parts.append((names, head_size + len(tables)))
                        tables += [picks, columns]
                    calls.append((p, kind, tuple(bunch), parts))
        chosen = lax.dynamic_slice(jnp.asarray(np.stack(tables)), (0, z, y), (len(tables), 1, 1)).reshape(-1)

        own = lax.dynamic_slice(mask_tiles, (z * row_tiles, y * col_tiles), (row_tiles, col_tiles))
        count = jnp.sum(own, axis=1)
        modes = jnp.where(count == col_tiles, FULL, jnp.where(count == 0, 0, SINGLE))
        single = jnp.argmax(own, axis=1)
        meta = jnp.concatenate([modes, single, jnp.reshape(mine, (1,)), chosen]).astype(jnp.int32)

        arrays = {"own": lower}
        rest = lower
        for p in range(poles):
            arrays[("own", p)] = rest[p]
            rest, arrays[("own", p)] = lax.optimization_barrier((rest, arrays[("own", p)]))

        queue = [[] for _ in range(final + 1)]
        sent_at = {}
        for call in calls:
            p, kind, bunch, parts = call
            t = max([ready.get(name, 0) for names, _ in parts for name in names])
            if kind == "send":
                sent_at.update({(p, i): t for i in bunch})
            else:
                t = min(max([t] + [sent_at[(p, i)] + 1 for i in bunch]), final)
            queue[t].append(call)

        late = {"meta": meta}
        state = {"panel": None, "part": {}, "sent": {}, "dens": {}}

        def run(call):
            p, kind, bunch, parts = call
            cfg = dict(
                name=f"{kind}_{p}_{bunch[0]}",
                kind=kind,
                last=kind == "keep" and p == end,
                parts=parts,
                pole=p,
                tile=tile,
                row_tiles=row_tiles,
                n_pole=n_pole,
                panel_width=group * width,
            )
            if kind == "send":
                made = slice_product(cfg, late["meta"], pole_weight, inverse, arrays, width)
                for i, part in zip(bunch, made):
                    state["part"][(p, i)] = part
                    state["sent"][(p, i)] = lax.ppermute(part, "row", [(0, 1), (1, 0)])
                return
            recv = [state["sent"][(p, i)] for i in bunch]
            panel, *shares = slice_product(
                cfg, late["meta"], pole_weight, inverse, arrays, width, recv, state["panel"]
            )
            state["panel"] = panel
            if shares:
                total = shares[0]
                for d in range(1, n_pole):
                    ways = [(q, (q + d) % n_pole) for q in range(n_pole)]
                    total = total + lax.ppermute(shares[d], "pole", ways).astype(jnp.float32)
                state["dens"][bunch[0]] = (total, meta[parts[0][1] + 1])

        def launch(kind, t, deps):
            if t >= len(lists[kind]):
                return
            name, moves = lists[kind][t]
            held = {}
            for zz, _, p, s0, s1 in moves:
                for yy, s in ((0, s0), (1, s1)):
                    held.setdefault(where[(zz, yy, p, s)], []).append((zz, yy))
            held = sorted(held.items(), key=lambda item: -len(item[1]))
            values = [arrays[source] for source, _ in held]
            values, state["panel"], _ = lax.optimization_barrier((values, state["panel"], deps))
            value = values[0]
            for other, (_, spots) in zip(values[1:], held[1:]):
                here = functools.reduce(jnp.logical_or, [(z == a) & (y == b) for a, b in spots])
                value = jnp.where(here, other, value)
            arrays[name] = lax.ppermute(value, "col", [(zz, to) for zz, to, *_ in moves])

        def landed(kind, t):
            return [arrays[lists[kind][t][0]]] if 0 <= t < len(lists[kind]) else []

        launch("out", 0, [])
        launch("across", 0, [])
        launch("in", 0, [])
        launch("out", 1, [])
        launch("across", 1, [])
        for t in range(final + 1):
            deps = landed("out", t)
            deps += [state["part"][key] for key, at in sent_at.items() if at == t - 1]
            deps += [state["sent"][key] for key, at in sent_at.items() if at == t - 2]
            launch("out", t + 2, deps)
            launch("across", t + 2, landed("out", t) + landed("across", t))
            launch("in", t + 1, landed("out", t - 1) + landed("in", t))
            for kind in ("send", "keep"):
                for call in queue[t]:
                    if call[1] == kind:
                        run(call)
                if t >= final - 2:
                    made = [state["part"][key] for key, at in sent_at.items() if at == t]
                    late["meta"], state["panel"], _ = lax.optimization_barrier((late["meta"], state["panel"], made))

        dens = state["dens"]
        columns = []
        for c in range(group):
            value = dens[0][0]
            for i in range(1, group):
                value = jnp.where(dens[i][1] == c, dens[i][0], value)
            columns.append(value)
        return (state["panel"], jnp.concatenate(columns, axis=1))

    return body


def solution(mesh):
    n_pole, n_row, n_col = (mesh.shape[name] for name in ("pole", "row", "col"))

    def whole(inverse, lower, mask_tiles, pole_weight):
        tile = inverse.shape[2] // mask_tiles.shape[0]
        width = lower.shape[3] // n_col
        rows = inverse.shape[2] // n_col
        fits = n_row == 2 and n_col % 2 == 0 and n_col > 2 and width % LANES == 0
        fits = fits and tile % LANES == 0 and rows % (16 * n_pole) == 0 and inverse.shape[0] > n_pole
        if fits:
            body = make_fast_body(n_col, n_pole, tile)
        else:
            body = functools.partial(general_body, tile)
        return jax.shard_map(
            body,
            mesh=mesh,
            in_specs=(
                P("pole", None, "col", "row"),
                P("pole", None, "row", "col"),
                P(),
                P("pole", None),
            ),
            out_specs=(P("pole", None, "col", "row"), P(("col", "pole"), "row")),
            check_vma=False,
        )(inverse, lower, mask_tiles, pole_weight)

    return whole
```

```python
import functools

import jax
import jax.numpy as jnp
import numpy as np
from jax import lax
from jax.experimental import pallas as pl
from jax.experimental.pallas import tpu as pltpu
from jax.sharding import PartitionSpec as P

ANY = pl.BlockSpec(memory_space=pl.ANY)
SMEM = pl.BlockSpec(memory_space=pltpu.SMEM)
LANES = 128
FULL, SINGLE = 2, 1


def complex_product(block, factors):
    real_part = jnp.einsum(
        "prc,pcw->prw", block[:, 0], factors[:, 0], preferred_element_type=jnp.float32
    ) - jnp.einsum("prc,pcw->prw", block[:, 1], factors[:, 1], preferred_element_type=jnp.float32)
    imag_part = jnp.einsum(
        "prc,pcw->prw", block[:, 0], factors[:, 1], preferred_element_type=jnp.float32
    ) + jnp.einsum("prc,pcw->prw", block[:, 1], factors[:, 0], preferred_element_type=jnp.float32)
    return jnp.stack([real_part, imag_part], axis=1)


def general_body(tile, inverse, lower, mask_tiles, pole_weight):
    full_lower = lax.all_gather(lower, "col", axis=3, tiled=True)
    row_tiles = inverse.shape[2] // tile
    col_tiles = inverse.shape[3] // tile
    start = (lax.axis_index("col") * row_tiles, lax.axis_index("row") * col_tiles)
    own = lax.dynamic_slice(mask_tiles, start, (row_tiles, col_tiles))
    keep = jnp.repeat(jnp.repeat(own, tile, axis=0), tile, axis=1).astype(inverse.dtype)
    partial_value = complex_product(inverse * keep[None, None], full_lower)
    summed = lax.psum_scatter(
        partial_value.astype(jnp.bfloat16), "row", scatter_dimension=3, tiled=True
    ).astype(jnp.float32)
    panel = (-summed).astype(jnp.bfloat16)
    values = panel.astype(jnp.float32)
    weighted = jnp.sum(
        pole_weight[:, 0, None, None] * values[:, 1] + pole_weight[:, 1, None, None] * values[:, 0],
        axis=0,
    )
    density = lax.psum_scatter(
        weighted.astype(jnp.bfloat16), "pole", scatter_dimension=0, tiled=True
    ).astype(jnp.float32)
    return (panel, density)


def slice_kernel(cfg, *refs):
    pole, tile, row_tiles, n_pole = (cfg[k] for k in ("pole", "tile", "row_tiles", "n_pole"))
    parts = cfg["parts"]
    n_parts = len(parts)
    keep, last = cfg["kind"] == "keep", cfg["last"]
    refs = list(refs)

    def take(count):
        taken = refs[:count]
        del refs[:count]
        return taken

    meta, weight, inv = take(3)
    cands = dict(zip(cfg["arrays"], take(len(cfg["arrays"]))))
    if keep:
        recv = take(n_parts)
        take(1 if cfg["aliased"] else 0)
    outs = take(1 if keep else n_parts)
    dens = take(n_pole if last else 0)
    abuf, wbuf, prod, obuf, asem, wsem, osem = take(7)
    width = wbuf.shape[1] // (2 * n_parts)
    depth = wbuf.shape[0]
    n_buf = abuf.shape[0]

    def start(copy):
        copy.start()

    def wait(copy):
        copy.wait()

    def tile_rows(r):
        return pl.ds(pl.multiple_of(r * tile, tile), tile)

    def fetch(r, act):
        slot = lax.rem(r, n_buf)

        @pl.when(meta[r] == FULL)
        def _():
            for c in range(2):
                act(pltpu.make_async_copy(inv.at[pole, c, tile_rows(r), :], abuf.at[slot, c], asem.at[slot, c]))

        @pl.when(meta[r] == SINGLE)
        def _():
            cols = tile_rows(meta[row_tiles + r])
            for c in range(2):
                act(
                    pltpu.make_async_copy(
                        inv.at[pole, c, tile_rows(r), cols], abuf.at[slot, c, :, pl.ds(0, tile)], asem.at[slot, c]
                    )
                )

    def lower_copies(j, ref):
        return [
            pltpu.make_async_copy(ref.at[h], wbuf.at[:, pl.ds((2 * j + h) * width, width)], wsem.at[j, h])
            for h in range(2)
        ]

    def source(name):
        return cands[name].at[pole] if name == "own" else cands[name]

    for j, (names, base) in enumerate(parts):
        for i, name in enumerate(names):

            @pl.when(meta[base] == i)
            def _(j=j, name=name):
                for copy in lower_copies(j, source(name)):
                    copy.start()

    fetch(0, start)
    columns = [pl.ds(pl.multiple_of(meta[base + 1] * width, width), width) for _, base in parts]
    extras = []
    if keep:
        rbuf, rsem = take(2)
        extras += [pltpu.make_async_copy(recv[j], rbuf.at[j], rsem.at[j]) for j in range(n_parts)]
    if last:
        pbuf, d32, d16, psem, dsem = take(5)
        extras += [
            pltpu.make_async_copy(outs[0].at[q, :, :, columns[0]], pbuf.at[q], psem.at[q]) for q in range(pole)
        ]
    for copy in extras:
        copy.start()
    for r in range(1, min(n_buf, row_tiles)):
        fetch(r, start)
    for j, (names, _) in enumerate(parts):
        for copy in lower_copies(j, source(names[0])):
            copy.wait()

    def out_copy(r, j):
        rows = tile_rows(r)
        target = outs[0].at[pole, :, rows, columns[j]] if keep else outs[j].at[:, rows, :]
        return pltpu.make_async_copy(obuf.at[j, :, rows, :], target, osem.at[r, j])

    def step(r, carry):
        slot = lax.rem(r, n_buf)
        rows = tile_rows(r)
        fetch(r, wait)

        @pl.when(meta[r] == FULL)
        def _():
            both = abuf[slot].reshape(2 * tile, depth)
            prod[...] = jnp.dot(both, wbuf[...], preferred_element_type=jnp.float32)

        @pl.when(meta[r] == SINGLE)
        def _():
            both = abuf[slot, :, :, :tile].reshape(2 * tile, tile)
            prod[...] = jnp.dot(both, wbuf[tile_rows(meta[row_tiles + r]), :], preferred_element_type=jnp.float32)

        @pl.when(meta[r] == 0)
        def _():
            prod[...] = jnp.zeros_like(prod)

        if extras:

            @pl.when(r == 0)
            def _():
                for copy in extras:
                    copy.wait()

        if row_tiles > n_buf:

            @pl.when(r + n_buf < row_tiles)
            def _():
                fetch(r + n_buf, start)

        for j in range(n_parts):
            low, high = (pl.ds((2 * j + h) * width, width) for h in range(2))
            re = prod[:tile, low] - prod[tile:, high]
            im = prod[:tile, high] + prod[tile:, low]
            if keep:
                re = -(re + rbuf[j, 0, rows, :].astype(jnp.float32))
                im = -(im + rbuf[j, 1, rows, :].astype(jnp.float32))
            re = re.astype(jnp.bfloat16)
            im = im.astype(jnp.bfloat16)
            obuf[j, 0, rows, :] = re
            obuf[j, 1, rows, :] = im
            out_copy(r, j).start()
        if last:
            total = weight[pole, 0] * im.astype(jnp.float32) + weight[pole, 1] * re.astype(jnp.float32)
            for q in range(pole):
                total = total + (
                    weight[q, 0] * pbuf[q, 1, rows, :].astype(jnp.float32)
                    + weight[q, 1] * pbuf[q, 0, rows, :].astype(jnp.float32)
                )
            d32[rows, :] = total
            d16[rows, :] = total.astype(jnp.bfloat16)
        return carry

    lax.fori_loop(0, row_tiles, step, 0)

    if last:
        share = d32.shape[0] // n_pole
        mine = meta[2 * row_tiles]
        copies = []
        for d in range(n_pole):
            block = lax.rem(mine + d, n_pole)
            rows = pl.ds(pl.multiple_of(block * share, share), share)
            copies.append(pltpu.make_async_copy((d16 if d else d32).at[rows, :], dens[d], dsem.at[d]))
        for copy in copies:
            copy.start()
        for copy in copies:
            copy.wait()

    def drain(r, carry):
        for j in range(n_parts):
            out_copy(r, j).wait()
        return carry

    lax.fori_loop(0, row_tiles, drain, 0)


def slice_product(cfg, meta, weight, inverse, arrays, width, recv=None, panel=None):
    poles, _, rows, depth = inverse.shape
    tile, row_tiles, n_pole, parts = cfg["tile"], cfg["row_tiles"], cfg["n_pole"], cfg["parts"]
    keep, last = cfg["kind"] == "keep", cfg["last"]
    n_buf = min(row_tiles, 4)
    n_parts = len(parts)
    names = sorted({name for part, _ in parts for name in part})
    part_shape = (2, rows, width)
    operands = [meta, weight, inverse, *(arrays[name] for name in names)]
    specs = [SMEM, SMEM] + [ANY] * (1 + len(names))
    aliases = {}
    outs = []
    if keep:
        operands += recv
        specs += [ANY] * n_parts
        outs.append(jax.ShapeDtypeStruct((poles, 2, rows, cfg["panel_width"]), jnp.bfloat16))
        if panel is not None:
            aliases = {len(operands): 0}
            operands.append(panel)
            specs.append(ANY)
    else:
        outs += [jax.ShapeDtypeStruct(part_shape, jnp.bfloat16)] * n_parts
    if last:
        share = rows // n_pole
        for d in range(n_pole):
            outs.append(jax.ShapeDtypeStruct((share, width), jnp.bfloat16 if d else jnp.float32))
    scratch = [
        pltpu.VMEM((n_buf, 2, tile, depth), jnp.bfloat16),
        pltpu.VMEM((depth, 2 * width * n_parts), jnp.bfloat16),
        pltpu.VMEM((2 * tile, 2 * width * n_parts), jnp.float32),
        pltpu.VMEM((n_parts, *part_shape), jnp.bfloat16),
        pltpu.SemaphoreType.DMA((n_buf, 2)),
        pltpu.SemaphoreType.DMA((n_parts, 2)),
        pltpu.SemaphoreType.DMA((row_tiles, n_parts)),
    ]
    if keep:
        scratch += [pltpu.VMEM((n_parts, *part_shape), jnp.bfloat16), pltpu.SemaphoreType.DMA((n_parts,))]
    if last:
        scratch += [
            pltpu.VMEM((max(poles - 1, 1), *part_shape), jnp.bfloat16),
            pltpu.VMEM((rows, width), jnp.float32),
            pltpu.VMEM((rows, width), jnp.bfloat16),
            pltpu.SemaphoreType.DMA((max(poles - 1, 1),)),
            pltpu.SemaphoreType.DMA((n_pole,)),
        ]
    cfg = dict(cfg, aliased=panel is not None, arrays=names)
    return pl.pallas_call(
        functools.partial(slice_kernel, cfg),
        out_shape=outs,
        in_specs=specs,
        out_specs=[ANY] * len(outs),
        scratch_shapes=scratch,
        input_output_aliases=aliases,
        compiler_params=pltpu.CompilerParams(vmem_limit_bytes=48 * 2**20),
        cost_estimate=pl.CostEstimate(flops=30 * rows * depth * n_parts, bytes_accessed=rows * width, transcendentals=0),
        name=cfg["name"],
    )(*operands)


def half_order(n_col, half, z):
    group = n_col // 2
    return sorted(range(half * group, (half + 1) * group), key=lambda s: abs(s - z))


def plan_transfers(n_col, poles):
    end, half = poles - 1, n_col // 2
    where = {(z, y, p, z): ("own", p) for z in range(n_col) for y in range(2) for p in range(poles)}
    lists = {"out": [], "across": [], "in": []}
    at = {}

    def add(kind, name, moves):
        moves = [m for m in moves if m[3] < n_col and m[4] < n_col]
        if not moves:
            return
        both = moves + [
            (n_col - 1 - z, n_col - 1 - to, p, n_col - 1 - s1, n_col - 1 - s0) for z, to, p, s0, s1 in moves
        ]
        for z, to, p, s0, s1 in both:
            where[(to, 0, p, s0)] = where[(to, 1, p, s1)] = name
        at[name] = len(lists[kind])
        lists[kind].append((name, both))

    def hop(z, p, step):
        return (z, z - 1, p, z + step - 1, z + step - 1)

    steps = range(1, n_col)
    pairs = [(p, step) for p in range(end) for step in steps]
    for p, step in sorted(pairs, key=lambda item: (item[0] * (n_col - 1) + item[1] - 3 * (item[1] == 1), item)):
        add("out", f"o{p}s{step}", [hop(z, p, step) for z in range(1, half)])
    natural = list(steps)
    turned = sorted(natural, key=lambda s: (s < half, s))
    for i, (a, b) in enumerate(zip(natural, turned)):
        far = [hop(z, end, i + 1) for z in range(2, half)]
        add("out", f"o{end}s{i + 1}", [(1, 0, end, b, a)] + [m for m in far if m[3] < n_col])
    for p in range(poles):
        for step in steps:
            add("across", f"a{p}s{step}", [hop(half, p, step)])
    for p in range(poles):
        for step in steps:
            add("in", f"i{p}s{step}", [hop(z, p, step) for z in range(half + 1, n_col)])
    return lists, where, at


def make_fast_body(n_col, n_pole, tile):
    group = n_col // 2
    places = [(zz, yy) for zz in range(n_col) for yy in range(2)]

    def body(inverse, lower, mask_tiles, pole_weight):
        poles, _, rows, depth = inverse.shape
        width = lower.shape[3]
        row_tiles, col_tiles = rows // tile, depth // tile
        end = poles - 1
        z, y, mine = lax.axis_index("col"), lax.axis_index("row"), lax.axis_index("pole")
        lists, where, ready = plan_transfers(n_col, poles)
        final = len(lists["out"]) - 1

        head_size = 2 * row_tiles + 1
        tables = []
        calls = []
        for p in range(poles):
            whole, single = [list(range(group))], [[i] for i in range(group)]
            for kind in ("send", "keep"):
                for bunch in single if p >= end - 1 else whole:
                    parts = []
                    for i in bunch:
                        names, picks, columns = [], np.zeros((n_col, 2), np.int32), np.zeros((n_col, 2), np.int32)
                        for zz, yy in places:
                            half = yy if kind == "keep" else 1 - yy
                            s = half_order(n_col, half, zz)[i]
                            name = where[(zz, yy, p, s)]
                            name = "own" if isinstance(name, tuple) else name
                            if name not in names:
                                names.append(name)
                            picks[zz, yy] = names.index(name)
                            columns[zz, yy] = s - half * group
                        parts.append((names, head_size + len(tables)))
                        tables += [picks, columns]
                    calls.append((p, kind, tuple(bunch), parts))
        chosen = lax.dynamic_slice(jnp.asarray(np.stack(tables)), (0, z, y), (len(tables), 1, 1)).reshape(-1)

        own = lax.dynamic_slice(mask_tiles, (z * row_tiles, y * col_tiles), (row_tiles, col_tiles))
        count = jnp.sum(own, axis=1)
        modes = jnp.where(count == col_tiles, FULL, jnp.where(count == 0, 0, SINGLE))
        single = jnp.argmax(own, axis=1)
        meta = jnp.concatenate([modes, single, jnp.reshape(mine, (1,)), chosen]).astype(jnp.int32)

        arrays = {"own": lower}
        rest = lower
        for p in range(poles):
            arrays[("own", p)] = rest[p]
            rest, arrays[("own", p)] = lax.optimization_barrier((rest, arrays[("own", p)]))

        queue = [[] for _ in range(final + 1)]
        sent_at = {}
        for call in calls:
            p, kind, bunch, parts = call
            t = max([ready.get(name, 0) for names, _ in parts for name in names])
            if kind == "send":
                sent_at.update({(p, i): t for i in bunch})
            else:
                t = min(max([t] + [sent_at[(p, i)] + 1 for i in bunch]), final)
            queue[t].append(call)

        late = {"meta": meta}
        state = {"panel": None, "part": {}, "sent": {}, "dens": {}}

        def run(call):
            p, kind, bunch, parts = call
            cfg = dict(
                name=f"{kind}_{p}_{bunch[0]}",
                kind=kind,
                last=kind == "keep" and p == end,
                parts=parts,
                pole=p,
                tile=tile,
                row_tiles=row_tiles,
                n_pole=n_pole,
                panel_width=group * width,
            )
            if kind == "send":
                made = slice_product(cfg, late["meta"], pole_weight, inverse, arrays, width)
                for i, part in zip(bunch, made):
                    state["part"][(p, i)] = part
                    state["sent"][(p, i)] = lax.ppermute(part, "row", [(0, 1), (1, 0)])
                return
            recv = [state["sent"][(p, i)] for i in bunch]
            panel, *shares = slice_product(
                cfg, late["meta"], pole_weight, inverse, arrays, width, recv, state["panel"]
            )
            state["panel"] = panel
            if shares:
                total = shares[0]
                for d in range(1, n_pole):
                    ways = [(q, (q + d) % n_pole) for q in range(n_pole)]
                    total = total + lax.ppermute(shares[d], "pole", ways).astype(jnp.float32)
                state["dens"][bunch[0]] = (total, meta[parts[0][1] + 1])

        def launch(kind, t, deps):
            if t >= len(lists[kind]):
                return
            name, moves = lists[kind][t]
            held = {}
            for zz, _, p, s0, s1 in moves:
                for yy, s in ((0, s0), (1, s1)):
                    held.setdefault(where[(zz, yy, p, s)], []).append((zz, yy))
            held = sorted(held.items(), key=lambda item: -len(item[1]))
            values = [arrays[source] for source, _ in held]
            values, state["panel"], _ = lax.optimization_barrier((values, state["panel"], deps))
            value = values[0]
            for other, (_, spots) in zip(values[1:], held[1:]):
                here = functools.reduce(jnp.logical_or, [(z == a) & (y == b) for a, b in spots])
                value = jnp.where(here, other, value)
            arrays[name] = lax.ppermute(value, "col", [(zz, to) for zz, to, *_ in moves])

        def landed(kind, t):
            return [arrays[lists[kind][t][0]]] if 0 <= t < len(lists[kind]) else []

        launch("out", 0, [])
        launch("across", 0, [])
        launch("in", 0, [])
        launch("out", 1, [])
        launch("across", 1, [])
        for t in range(final + 1):
            deps = landed("out", t)
            deps += [state["part"][key] for key, at in sent_at.items() if at == t - 1]
            deps += [state["sent"][key] for key, at in sent_at.items() if at == t - 2]
            launch("out", t + 2, deps)
            launch("across", t + 2, landed("out", t) + landed("across", t))
            launch("in", t + 1, landed("out", t - 1) + landed("in", t))
            for kind in ("send", "keep"):
                for call in queue[t]:
                    if call[1] == kind:
                        run(call)
                if t >= final - 2:
                    made = [state["part"][key] for key, at in sent_at.items() if at == t]
                    late["meta"], state["panel"], _ = lax.optimization_barrier((late["meta"], state["panel"], made))

        dens = state["dens"]
        columns = []
        for c in range(group):
            value = dens[0][0]
            for i in range(1, group):
                value = jnp.where(dens[i][1] == c, dens[i][0], value)
            columns.append(value)
        return (state["panel"], jnp.concatenate(columns, axis=1))

    return body


def solution(mesh):
    n_pole, n_row, n_col = (mesh.shape[name] for name in ("pole", "row", "col"))

    def whole(inverse, lower, mask_tiles, pole_weight):
        tile = inverse.shape[2] // mask_tiles.shape[0]
        width = lower.shape[3] // n_col
        rows = inverse.shape[2] // n_col
        fits = n_row == 2 and n_col % 2 == 0 and n_col > 2 and width % LANES == 0
        fits = fits and tile % LANES == 0 and rows % (16 * n_pole) == 0 and inverse.shape[0] > n_pole
        if fits:
            body = make_fast_body(n_col, n_pole, tile)
        else:
            body = functools.partial(general_body, tile)
        return jax.shard_map(
            body,
            mesh=mesh,
            in_specs=(
                P("pole", None, "col", "row"),
                P("pole", None, "row", "col"),
                P(),
                P("pole", None),
            ),
            out_specs=(P("pole", None, "col", "row"), P(("col", "pole"), "row")),
            check_vma=False,
        )(inverse, lower, mask_tiles, pole_weight)

    return whole
```

```python
import functools

import jax
import jax.numpy as jnp
import numpy as np
from jax import lax
from jax.experimental import pallas as pl
from jax.experimental.pallas import tpu as pltpu
from jax.sharding import PartitionSpec as P

ANY = pl.BlockSpec(memory_space=pl.ANY)
SMEM = pl.BlockSpec(memory_space=pltpu.SMEM)
LANES = 128
FULL, SINGLE = 2, 1


def complex_product(block, factors):
    real_part = jnp.einsum(
        "prc,pcw->prw", block[:, 0], factors[:, 0], preferred_element_type=jnp.float32
    ) - jnp.einsum("prc,pcw->prw", block[:, 1], factors[:, 1], preferred_element_type=jnp.float32)
    imag_part = jnp.einsum(
        "prc,pcw->prw", block[:, 0], factors[:, 1], preferred_element_type=jnp.float32
    ) + jnp.einsum("prc,pcw->prw", block[:, 1], factors[:, 0], preferred_element_type=jnp.float32)
    return jnp.stack([real_part, imag_part], axis=1)


def general_body(tile, inverse, lower, mask_tiles, pole_weight):
    full_lower = lax.all_gather(lower, "col", axis=3, tiled=True)
    row_tiles = inverse.shape[2] // tile
    col_tiles = inverse.shape[3] // tile
    start = (lax.axis_index("col") * row_tiles, lax.axis_index("row") * col_tiles)
    own = lax.dynamic_slice(mask_tiles, start, (row_tiles, col_tiles))
    keep = jnp.repeat(jnp.repeat(own, tile, axis=0), tile, axis=1).astype(inverse.dtype)
    partial_value = complex_product(inverse * keep[None, None], full_lower)
    summed = lax.psum_scatter(
        partial_value.astype(jnp.bfloat16), "row", scatter_dimension=3, tiled=True
    ).astype(jnp.float32)
    panel = (-summed).astype(jnp.bfloat16)
    values = panel.astype(jnp.float32)
    weighted = jnp.sum(
        pole_weight[:, 0, None, None] * values[:, 1] + pole_weight[:, 1, None, None] * values[:, 0],
        axis=0,
    )
    density = lax.psum_scatter(
        weighted.astype(jnp.bfloat16), "pole", scatter_dimension=0, tiled=True
    ).astype(jnp.float32)
    return (panel, density)


def slice_kernel(cfg, *refs):
    pole, tile, row_tiles, n_pole = (cfg[k] for k in ("pole", "tile", "row_tiles", "n_pole"))
    parts = cfg["parts"]
    n_parts = len(parts)
    keep, fold, last = cfg["kind"] == "keep", cfg["kind"] == "fold", cfg["last"]
    low_tile, n_tiles = cfg["span"]
    folded = low_tile > 0
    span = pl.ds(low_tile * tile, n_tiles * tile)
    refs = list(refs)

    def take(count):
        taken = refs[:count]
        del refs[:count]
        return taken

    meta, weight, inv = take(3)
    cands = dict(zip(cfg["arrays"], take(len(cfg["arrays"]))))
    if keep:
        recv = take(n_parts)
        earlier = take(2 if folded else 0)
        take(1 if cfg["aliased"] else 0)
    if fold:
        (panel,) = take(1)
    outs = take(2 if fold else 1 if keep else n_parts)
    if keep:
        (panel,) = outs
    dens = take(n_pole if last else 0)
    abuf, wbuf, prod, obuf, asem, wsem, osem = take(7)
    width = wbuf.shape[1] // (2 * n_parts)
    depth = wbuf.shape[0]
    n_buf = abuf.shape[0]

    def start(copy):
        copy.start()

    def wait(copy):
        copy.wait()

    def tile_rows(r):
        return pl.ds(pl.multiple_of(r * tile, tile), tile)

    def single(r):
        at = meta[row_tiles + r]
        return (meta[r] == SINGLE) & (at >= low_tile) & (at < low_tile + n_tiles)

    def fetch(r, act):
        slot = lax.rem(r, n_buf)

        @pl.when(meta[r] == FULL)
        def _():
            for c in range(2):
                act(pltpu.make_async_copy(inv.at[pole, c, tile_rows(r), span], abuf.at[slot, c], asem.at[slot, c]))

        @pl.when(single(r))
        def _():
            cols = tile_rows(meta[row_tiles + r])
            for c in range(2):
                act(
                    pltpu.make_async_copy(
                        inv.at[pole, c, tile_rows(r), cols], abuf.at[slot, c, :, pl.ds(0, tile)], asem.at[slot, c]
                    )
                )

    def lower_copies(j, ref):
        return [
            pltpu.make_async_copy(ref[h], wbuf.at[:, pl.ds((2 * j + h) * width, width)], wsem.at[j, h])
            for h in range(2)
        ]

    def source(name):
        whole = cands[name].at[pole] if name == "own" else cands[name]
        return [whole.at[h] if name in cfg["cut"] else whole.at[h, span, :] for h in range(2)]

    for j, (names, base) in enumerate(parts):
        for i, name in enumerate(names):

            @pl.when(meta[base] == i)
            def _(j=j, name=name):
                for copy in lower_copies(j, source(name)):
                    copy.start()

    fetch(0, start)
    columns = [pl.ds(pl.multiple_of(meta[base + 1] * width, width), width) for _, base in parts]
    extras = []
    if keep:
        rbuf, rsem = take(2)
        extras += [pltpu.make_async_copy(recv[j], rbuf.at[j], rsem.at[j]) for j in range(n_parts)]
    if fold or (last and not folded):
        pbuf, psem = take(2)
        extras += [
            pltpu.make_async_copy(panel.at[q, :, :, columns[0]], pbuf.at[q], psem.at[q]) for q in range(pole)
        ]
    if last and folded:
        held, hsem = take(2)
        base, bsem = take(2)
        extras += [pltpu.make_async_copy(earlier[0], held, hsem), pltpu.make_async_copy(earlier[1], base, bsem)]
    if last:
        d32, d16, dsem = take(3)
    for copy in extras:
        copy.start()
    for r in range(1, min(n_buf, row_tiles)):
        fetch(r, start)
    for j, (names, _) in enumerate(parts):
        for copy in lower_copies(j, source(names[0])):
            copy.wait()

    def out_copy(r, j):
        rows = tile_rows(r)
        target = panel.at[pole, :, rows, columns[j]] if keep else outs[j].at[:, rows, :]
        return pltpu.make_async_copy(obuf.at[j, :, rows, :], target, osem.at[r, j])

    def sum_copy(r):
        return pltpu.make_async_copy(sbuf.at[tile_rows(r), :], outs[1].at[tile_rows(r), :], ssem.at[r])

    def other_poles(rows):
        return sum(
            weight[q, 0] * pbuf[q, 1, rows, :].astype(jnp.float32)
            + weight[q, 1] * pbuf[q, 0, rows, :].astype(jnp.float32)
            for q in range(pole)
        )

    if fold:
        sbuf, ssem = take(2)

    def step(r, carry):
        slot = lax.rem(r, n_buf)
        rows = tile_rows(r)
        fetch(r, wait)

        @pl.when(meta[r] == FULL)
        def _():
            both = abuf[slot].reshape(2 * tile, n_tiles * tile)
            prod[...] = jnp.dot(both, wbuf[...], preferred_element_type=jnp.float32)

        @pl.when(single(r))
        def _():
            both = abuf[slot, :, :, :tile].reshape(2 * tile, tile)
            prod[...] = jnp.dot(both, wbuf[tile_rows(meta[row_tiles + r] - low_tile), :], preferred_element_type=jnp.float32)

        @pl.when((meta[r] != FULL) & jnp.logical_not(single(r)))
        def _():
            prod[...] = jnp.zeros_like(prod)

        if extras:

            @pl.when(r == 0)
            def _():
                for copy in extras:
                    copy.wait()

        if row_tiles > n_buf:

            @pl.when(r + n_buf < row_tiles)
            def _():
                fetch(r + n_buf, start)

        for j in range(n_parts):
            low, high = (pl.ds((2 * j + h) * width, width) for h in range(2))
            re = prod[:tile, low] - prod[tile:, high]
            im = prod[:tile, high] + prod[tile:, low]
            if keep:
                re = re + rbuf[j, 0, rows, :].astype(jnp.float32)
                im = im + rbuf[j, 1, rows, :].astype(jnp.float32)
                if folded:
                    re = re + held[0, rows, :]
                    im = im + held[1, rows, :]
                re, im = -re, -im
            re = re.astype(obuf.dtype)
            im = im.astype(obuf.dtype)
            obuf[j, 0, rows, :] = re
            obuf[j, 1, rows, :] = im
            out_copy(r, j).start()
        if last:
            total = weight[pole, 0] * im.astype(jnp.float32) + weight[pole, 1] * re.astype(jnp.float32)
            total = total + (base[rows, :] if folded else other_poles(rows))
            d32[rows, :] = total
            d16[rows, :] = total.astype(jnp.bfloat16)
        if fold:
            sbuf[rows, :] = other_poles(rows)
            sum_copy(r).start()
        return carry

    lax.fori_loop(0, row_tiles, step, 0)

    if last:
        share = d32.shape[0] // n_pole
        mine = meta[2 * row_tiles]
        copies = []
        for d in range(n_pole):
            block = lax.rem(mine + d, n_pole)
            rows = pl.ds(pl.multiple_of(block * share, share), share)
            copies.append(pltpu.make_async_copy((d16 if d else d32).at[rows, :], dens[d], dsem.at[d]))
        for copy in copies:
            copy.start()
        for copy in copies:
            copy.wait()

    def drain(r, carry):
        for j in range(n_parts):
            out_copy(r, j).wait()
        if fold:
            sum_copy(r).wait()
        return carry

    lax.fori_loop(0, row_tiles, drain, 0)


def slice_product(cfg, meta, weight, inverse, arrays, width, recv=None, panel=None, earlier=()):
    poles, _, rows, _ = inverse.shape
    tile, row_tiles, n_pole, parts = cfg["tile"], cfg["row_tiles"], cfg["n_pole"], cfg["parts"]
    keep, fold, last = cfg["kind"] == "keep", cfg["kind"] == "fold", cfg["last"]
    n_buf = min(row_tiles, 4)
    depth = cfg["span"][1] * tile
    n_parts = len(parts)
    names = sorted({name for part, _ in parts for name in part})
    part_shape = (2, rows, width)
    operands = [meta, weight, inverse, *(arrays[name] for name in names)]
    specs = [SMEM, SMEM] + [ANY] * (1 + len(names))
    aliases = {}
    outs = []
    if keep:
        operands += [*recv, *earlier]
        specs += [ANY] * (n_parts + len(earlier))
        outs.append(jax.ShapeDtypeStruct((poles, 2, rows, cfg["panel_width"]), jnp.bfloat16))
        if panel is not None:
            aliases = {len(operands): 0}
            operands.append(panel)
            specs.append(ANY)
    elif fold:
        operands.append(panel)
        specs.append(ANY)
        outs += [jax.ShapeDtypeStruct(part_shape, jnp.float32), jax.ShapeDtypeStruct((rows, width), jnp.float32)]
    else:
        outs += [jax.ShapeDtypeStruct(part_shape, jnp.bfloat16)] * n_parts
    if last:
        share = rows // n_pole
        for d in range(n_pole):
            outs.append(jax.ShapeDtypeStruct((share, width), jnp.bfloat16 if d else jnp.float32))
    scratch = [
        pltpu.VMEM((n_buf, 2, tile, depth), jnp.bfloat16),
        pltpu.VMEM((depth, 2 * width * n_parts), jnp.bfloat16),
        pltpu.VMEM((2 * tile, 2 * width * n_parts), jnp.float32),
        pltpu.VMEM((n_parts, *part_shape), jnp.float32 if fold else jnp.bfloat16),
        pltpu.SemaphoreType.DMA((n_buf, 2)),
        pltpu.SemaphoreType.DMA((n_parts, 2)),
        pltpu.SemaphoreType.DMA((row_tiles, n_parts)),
    ]
    if keep:
        scratch += [pltpu.VMEM((n_parts, *part_shape), jnp.bfloat16), pltpu.SemaphoreType.DMA((n_parts,))]
    if fold or (last and not earlier):
        scratch += [
            pltpu.VMEM((max(poles - 1, 1), *part_shape), jnp.bfloat16),
            pltpu.SemaphoreType.DMA((max(poles - 1, 1),)),
        ]
    if last and earlier:
        scratch += [pltpu.VMEM(part_shape, jnp.float32), pltpu.SemaphoreType.DMA]
        scratch += [pltpu.VMEM((rows, width), jnp.float32), pltpu.SemaphoreType.DMA]
    if last:
        scratch += [
            pltpu.VMEM((rows, width), jnp.float32),
            pltpu.VMEM((rows, width), jnp.bfloat16),
            pltpu.SemaphoreType.DMA((n_pole,)),
        ]
    if fold:
        scratch += [pltpu.VMEM((rows, width), jnp.float32), pltpu.SemaphoreType.DMA((row_tiles,))]
    cfg = dict(cfg, aliased=panel is not None, arrays=names)
    return pl.pallas_call(
        functools.partial(slice_kernel, cfg),
        out_shape=outs,
        in_specs=specs,
        out_specs=[ANY] * len(outs),
        scratch_shapes=scratch,
        input_output_aliases=aliases,
        compiler_params=pltpu.CompilerParams(vmem_limit_bytes=48 * 2**20),
        cost_estimate=pl.CostEstimate(flops=30 * rows * depth * n_parts, bytes_accessed=rows * width, transcendentals=0),
        name=cfg["name"],
    )(*operands)


def half_order(n_col, half, z):
    group = n_col // 2
    return sorted(range(half * group, (half + 1) * group), key=lambda s: abs(s - z))


def plan_transfers(n_col, poles):
    end, half = poles - 1, n_col // 2
    where = {(z, y, p, z): ("own", p) for z in range(n_col) for y in range(2) for p in range(poles)}
    lists = {"out": [], "across": [], "in": []}
    at = {}

    def add(kind, name, moves):
        moves = [m for m in moves if m[3] < n_col and m[4] < n_col]
        if not moves:
            return
        both = moves + [
            (n_col - 1 - z, n_col - 1 - to, p, n_col - 1 - s1, n_col - 1 - s0) for z, to, p, s0, s1 in moves
        ]
        for z, to, p, s0, s1 in both:
            where[(to, 0, p, s0)] = where[(to, 1, p, s1)] = name
        at[name] = len(lists[kind])
        lists[kind].append((name, both))

    def hop(z, p, step):
        return (z, z - 1, p, z + step - 1, z + step - 1)

    steps = range(1, n_col)
    pairs = [(p, step) for p in range(end) for step in steps]
    for p, step in sorted(pairs, key=lambda item: (item[0] * (n_col - 1) + item[1] - 3 * (item[1] == 1), item)):
        add("out", f"o{p}s{step}", [hop(z, p, step) for z in range(1, half)])
    natural = list(steps)
    turned = sorted(natural, key=lambda s: (s < half, s))
    for i, (a, b) in enumerate(zip(natural, turned)):
        far = [hop(z, end, i + 1) for z in range(2, half)]
        add("out", f"o{end}s{i + 1}", [(1, 0, end, b, a)] + [m for m in far if m[3] < n_col])
    for p in range(poles):
        for step in steps:
            add("across", f"a{p}s{step}", [hop(half, p, step)])
    for p in range(poles):
        for step in steps:
            add("in", f"i{p}s{step}", [hop(z, p, step) for z in range(half + 1, n_col)])
    return lists, where, at


def make_fast_body(n_col, n_pole, tile):
    group = n_col // 2
    places = [(zz, yy) for zz in range(n_col) for yy in range(2)]

    def body(inverse, lower, mask_tiles, pole_weight):
        poles, _, rows, depth = inverse.shape
        width = lower.shape[3]
        row_tiles, col_tiles = rows // tile, depth // tile
        end = poles - 1
        z, y, mine = lax.axis_index("col"), lax.axis_index("row"), lax.axis_index("pole")
        lists, where, ready = plan_transfers(n_col, poles)
        final = len(lists["out"]) - 1
        final_name = lists["out"][final][0]
        cuts = col_tiles - max(1, 3 * col_tiles // 8) if col_tiles > 1 and poles > 1 else 0

        head_size = 2 * row_tiles + 1
        tables = []
        calls = []
        for p in range(poles):
            whole, single = [list(range(group))], [[i] for i in range(group)]
            for kind in ("send", "keep"):
                for bunch in single if p >= end - 1 else whole:
                    parts = []
                    for i in bunch:
                        names, picks, columns = [], np.zeros((n_col, 2), np.int32), np.zeros((n_col, 2), np.int32)
                        for zz, yy in places:
                            half = yy if kind == "keep" else 1 - yy
                            s = half_order(n_col, half, zz)[i]
                            name = where[(zz, yy, p, s)]
                            name = "own" if isinstance(name, tuple) else name
                            if name not in names:
                                names.append(name)
                            picks[zz, yy] = names.index(name)
                            columns[zz, yy] = s - half * group
                        parts.append((names, head_size + len(tables)))
                        tables += [picks, columns]
                    calls.append((p, kind, tuple(bunch), parts))
        chosen = lax.dynamic_slice(jnp.asarray(np.stack(tables)), (0, z, y), (len(tables), 1, 1)).reshape(-1)

        own = lax.dynamic_slice(mask_tiles, (z * row_tiles, y * col_tiles), (row_tiles, col_tiles))
        count = jnp.sum(own, axis=1)
        modes = jnp.where(count == col_tiles, FULL, jnp.where(count == 0, 0, SINGLE))
        single = jnp.argmax(own, axis=1)
        meta = jnp.concatenate([modes, single, jnp.reshape(mine, (1,)), chosen]).astype(jnp.int32)

        arrays = {"own": lower}
        rest = lower
        for p in range(poles):
            arrays[("own", p)] = rest[p]
            rest, arrays[("own", p)] = lax.optimization_barrier((rest, arrays[("own", p)]))

        queue = [[] for _ in range(final + 1)]
        sent_at = {}
        for call in calls:
            p, kind, bunch, parts = call
            t = max([ready.get(name, 0) for names, _ in parts for name in names])
            if kind == "send":
                sent_at.update({(p, i): t for i in bunch})
            else:
                t = min(max([t] + [sent_at[(p, i)] + 1 for i in bunch]), final)
            queue[t].append(call)

        late = {"meta": meta}
        state = {"panel": None, "part": {}, "sent": {}, "dens": {}}

        def run(call):
            p, kind, bunch, parts = call
            cfg = dict(
                name=f"{kind}_{p}_{bunch[0]}",
                kind=kind,
                last=kind == "keep" and p == end,
                parts=parts,
                pole=p,
                tile=tile,
                row_tiles=row_tiles,
                n_pole=n_pole,
                panel_width=group * width,
                span=(0, col_tiles),
                cut=[],
            )
            if kind == "send":
                made = slice_product(cfg, late["meta"], pole_weight, inverse, arrays, width)
                for i, part in zip(bunch, made):
                    state["part"][(p, i)] = part
                    state["sent"][(p, i)] = lax.ppermute(part, "row", [(0, 1), (1, 0)])
                return
            recv = [state["sent"][(p, i)] for i in bunch]
            sources, earlier = arrays, ()
            if cuts and final_name in parts[0][0]:
                sources = dict(arrays, **{final_name: arrays[final_name][0]})
                first = dict(cfg, name=f"fold_{p}_{bunch[0]}", kind="fold", last=False, span=(0, cuts), cut=[final_name])
                earlier = slice_product(
                    first, late["meta"], pole_weight, inverse, sources, width, panel=state["panel"]
                )
                sources = dict(arrays, **{final_name: arrays[final_name][1]})
                cfg.update(span=(cuts, col_tiles - cuts), cut=[final_name])
            panel, *shares = slice_product(
                cfg, late["meta"], pole_weight, inverse, sources, width, recv, state["panel"], earlier
            )
            state["panel"] = panel
            if shares:
                total = shares[0]
                for d in range(1, n_pole):
                    ways = [(q, (q + d) % n_pole) for q in range(n_pole)]
                    total = total + lax.ppermute(shares[d], "pole", ways).astype(jnp.float32)
                state["dens"][bunch[0]] = total

        def is_one_of(spots):
            return functools.reduce(jnp.logical_or, [(z == a) & (y == b) for a, b in spots])

        def launch(kind, t, deps):
            if t >= len(lists[kind]):
                return
            name, moves = lists[kind][t]
            held = {}
            for zz, _, p, s0, s1 in moves:
                for yy, s in ((0, s0), (1, s1)):
                    held.setdefault(where[(zz, yy, p, s)], []).append((zz, yy))
            held = sorted(held.items(), key=lambda item: -len(item[1]))
            values = [arrays[source] for source, _ in held]
            values, state["panel"], _ = lax.optimization_barrier((values, state["panel"], deps))
            value = values[0]
            for other, (_, spots) in zip(values[1:], held[1:]):
                value = jnp.where(is_one_of(spots), other, value)
            ways = [(zz, to) for zz, to, *_ in moves]
            if name == final_name and cuts:
                pieces = [value[:, : cuts * tile], value[:, cuts * tile :]]
                arrays[name] = [lax.ppermute(piece, "col", ways) for piece in pieces]
            else:
                arrays[name] = lax.ppermute(value, "col", ways)

        def landed(kind, t):
            return [arrays[lists[kind][t][0]]] if 0 <= t < len(lists[kind]) else []

        launch("out", 0, [])
        launch("across", 0, [])
        launch("in", 0, [])
        launch("out", 1, [])
        launch("across", 1, [])
        for t in range(final + 1):
            deps = landed("out", t)
            deps += [state["part"][key] for key, at in sent_at.items() if at == t - 1]
            deps += [state["sent"][key] for key, at in sent_at.items() if at == t - 2]
            launch("out", t + 2, deps)
            launch("across", t + 2, landed("out", t) + landed("across", t))
            launch("in", t + 1, landed("out", t) + landed("in", t))
            for kind in ("send", "keep"):
                for call in queue[t]:
                    if call[1] == kind:
                        run(call)
                if t >= final - 2:
                    made = [state["part"][key] for key, at in sent_at.items() if at == t]
                    late["meta"], state["panel"], _ = lax.optimization_barrier((late["meta"], state["panel"], made))

        dens = state["dens"]
        columns = []
        for c in range(group):
            value = dens[0]
            for i in range(1, group):
                spots = [(a, b) for a, b in places if half_order(n_col, b, a)[i] - b * group == c]
                value = jnp.where(is_one_of(spots), dens[i], value)
            columns.append(value)
        return (state["panel"], jnp.concatenate(columns, axis=1))

    return body


def solution(mesh):
    n_pole, n_row, n_col = (mesh.shape[name] for name in ("pole", "row", "col"))

    def whole(inverse, lower, mask_tiles, pole_weight):
        tile = inverse.shape[2] // mask_tiles.shape[0]
        width = lower.shape[3] // n_col
        rows = inverse.shape[2] // n_col
        fits = n_row == 2 and n_col % 2 == 0 and n_col > 2 and width % LANES == 0
        fits = fits and tile % LANES == 0 and rows % (16 * n_pole) == 0 and inverse.shape[0] > n_pole
        if fits:
            body = make_fast_body(n_col, n_pole, tile)
        else:
            body = functools.partial(general_body, tile)
        return jax.shard_map(
            body,
            mesh=mesh,
            in_specs=(
                P("pole", None, "col", "row"),
                P("pole", None, "row", "col"),
                P(),
                P("pole", None),
            ),
            out_specs=(P("pole", None, "col", "row"), P(("col", "pole"), "row")),
            check_vma=False,
        )(inverse, lower, mask_tiles, pole_weight)

    return whole
```

```python
import functools

import jax
import jax.numpy as jnp
import numpy as np
from jax import lax
from jax.experimental import pallas as pl
from jax.experimental.pallas import tpu as pltpu
from jax.sharding import PartitionSpec as P

ANY = pl.BlockSpec(memory_space=pl.ANY)
SMEM = pl.BlockSpec(memory_space=pltpu.SMEM)
LANES = 128
FULL, SINGLE = 2, 1


def complex_product(block, factors):
    real_part = jnp.einsum(
        "prc,pcw->prw", block[:, 0], factors[:, 0], preferred_element_type=jnp.float32
    ) - jnp.einsum("prc,pcw->prw", block[:, 1], factors[:, 1], preferred_element_type=jnp.float32)
    imag_part = jnp.einsum(
        "prc,pcw->prw", block[:, 0], factors[:, 1], preferred_element_type=jnp.float32
    ) + jnp.einsum("prc,pcw->prw", block[:, 1], factors[:, 0], preferred_element_type=jnp.float32)
    return jnp.stack([real_part, imag_part], axis=1)


def general_body(tile, inverse, lower, mask_tiles, pole_weight):
    full_lower = lax.all_gather(lower, "col", axis=3, tiled=True)
    row_tiles = inverse.shape[2] // tile
    col_tiles = inverse.shape[3] // tile
    start = (lax.axis_index("col") * row_tiles, lax.axis_index("row") * col_tiles)
    own = lax.dynamic_slice(mask_tiles, start, (row_tiles, col_tiles))
    keep = jnp.repeat(jnp.repeat(own, tile, axis=0), tile, axis=1).astype(inverse.dtype)
    partial_value = complex_product(inverse * keep[None, None], full_lower)
    summed = lax.psum_scatter(
        partial_value.astype(jnp.bfloat16), "row", scatter_dimension=3, tiled=True
    ).astype(jnp.float32)
    panel = (-summed).astype(jnp.bfloat16)
    values = panel.astype(jnp.float32)
    weighted = jnp.sum(
        pole_weight[:, 0, None, None] * values[:, 1] + pole_weight[:, 1, None, None] * values[:, 0],
        axis=0,
    )
    density = lax.psum_scatter(
        weighted.astype(jnp.bfloat16), "pole", scatter_dimension=0, tiled=True
    ).astype(jnp.float32)
    return (panel, density)


def slice_kernel(cfg, *refs):
    pole, tile, row_tiles, n_pole = (cfg[k] for k in ("pole", "tile", "row_tiles", "n_pole"))
    parts = cfg["parts"]
    n_parts = len(parts)
    keep, fold, last = cfg["kind"] == "keep", cfg["kind"] == "fold", cfg["last"]
    low_tile, n_tiles = cfg["span"]
    folded = low_tile > 0
    span = pl.ds(low_tile * tile, n_tiles * tile)
    refs = list(refs)

    def take(count):
        taken = refs[:count]
        del refs[:count]
        return taken

    meta, weight, inv = take(3)
    cands = dict(zip(cfg["arrays"], take(len(cfg["arrays"]))))
    if keep:
        recv = take(n_parts)
        earlier = take(2 if folded else 0)
        take(cfg["aliased"])
    if fold:
        (panel,) = take(1)
    outs = take(2 if fold else 1 if keep else n_parts)
    if keep:
        (panel,) = outs
    dens = take(n_pole if last else 0)
    abuf, wbuf, prod, obuf, asem, wsem, osem = take(7)
    width = wbuf.shape[1] // (2 * n_parts)
    depth = wbuf.shape[0]
    n_buf = abuf.shape[0]

    def start(copy):
        copy.start()

    def wait(copy):
        copy.wait()

    def tile_rows(r):
        return pl.ds(pl.multiple_of(r * tile, tile), tile)

    def single(r):
        at = meta[row_tiles + r]
        return (meta[r] == SINGLE) & (at >= low_tile) & (at < low_tile + n_tiles)

    def fetch(r, act):
        slot = lax.rem(r, n_buf)

        @pl.when(meta[r] == FULL)
        def _():
            for c in range(2):
                act(pltpu.make_async_copy(inv.at[pole, c, tile_rows(r), span], abuf.at[slot, c], asem.at[slot, c]))

        @pl.when(single(r))
        def _():
            cols = tile_rows(meta[row_tiles + r])
            for c in range(2):
                act(
                    pltpu.make_async_copy(
                        inv.at[pole, c, tile_rows(r), cols], abuf.at[slot, c, :, pl.ds(0, tile)], asem.at[slot, c]
                    )
                )

    def lower_copies(j, ref):
        return [
            pltpu.make_async_copy(ref[h], wbuf.at[:, pl.ds((2 * j + h) * width, width)], wsem.at[j, h])
            for h in range(2)
        ]

    def source(name):
        whole = cands[name].at[pole] if name == "own" else cands[name]
        return [whole.at[h] if name in cfg["cut"] else whole.at[h, span, :] for h in range(2)]

    for j, (names, base) in enumerate(parts):
        for i, name in enumerate(names):

            @pl.when(meta[base] == i)
            def _(j=j, name=name):
                for copy in lower_copies(j, source(name)):
                    copy.start()

    fetch(0, start)
    columns = [pl.ds(pl.multiple_of(meta[base + 1] * width, width), width) for _, base in parts]
    extras = []
    if keep:
        rbuf, rsem = take(2)
        extras += [pltpu.make_async_copy(recv[j], rbuf.at[j], rsem.at[j]) for j in range(n_parts)]
    if fold or (last and not folded):
        pbuf, psem = take(2)
        extras += [
            pltpu.make_async_copy(panel.at[q, :, :, columns[0]], pbuf.at[q], psem.at[q]) for q in range(pole)
        ]
    if last and folded:
        held, hsem = take(2)
        base, bsem = take(2)
        extras += [pltpu.make_async_copy(earlier[0], held, hsem), pltpu.make_async_copy(earlier[1], base, bsem)]
    if last:
        d32, d16, dsem = take(3)
    for copy in extras:
        copy.start()
    for r in range(1, min(n_buf, row_tiles)):
        fetch(r, start)
    for j, (names, _) in enumerate(parts):
        for copy in lower_copies(j, source(names[0])):
            copy.wait()

    def out_copy(r, j):
        rows = tile_rows(r)
        target = panel.at[pole, :, rows, columns[j]] if keep else outs[j].at[:, rows, :]
        return pltpu.make_async_copy(obuf.at[j, :, rows, :], target, osem.at[r, j])

    def sum_copy(r):
        return pltpu.make_async_copy(sbuf.at[tile_rows(r), :], outs[1].at[tile_rows(r), :], ssem.at[r])

    def other_poles(rows):
        return sum(
            weight[q, 0] * pbuf[q, 1, rows, :].astype(jnp.float32)
            + weight[q, 1] * pbuf[q, 0, rows, :].astype(jnp.float32)
            for q in range(pole)
        )

    if fold:
        sbuf, ssem = take(2)

    def step(r, carry):
        slot = lax.rem(r, n_buf)
        rows = tile_rows(r)
        fetch(r, wait)

        @pl.when(meta[r] == FULL)
        def _():
            both = abuf[slot].reshape(2 * tile, n_tiles * tile)
            prod[...] = jnp.dot(both, wbuf[...], preferred_element_type=jnp.float32)

        @pl.when(single(r))
        def _():
            both = abuf[slot, :, :, :tile].reshape(2 * tile, tile)
            prod[...] = jnp.dot(both, wbuf[tile_rows(meta[row_tiles + r] - low_tile), :], preferred_element_type=jnp.float32)

        @pl.when((meta[r] != FULL) & jnp.logical_not(single(r)))
        def _():
            prod[...] = jnp.zeros_like(prod)

        if extras:

            @pl.when(r == 0)
            def _():
                for copy in extras:
                    copy.wait()

        if row_tiles > n_buf:

            @pl.when(r + n_buf < row_tiles)
            def _():
                fetch(r + n_buf, start)

        for j in range(n_parts):
            low, high = (pl.ds((2 * j + h) * width, width) for h in range(2))
            re = prod[:tile, low] - prod[tile:, high]
            im = prod[:tile, high] + prod[tile:, low]
            if keep:
                re = re + rbuf[j, 0, rows, :].astype(jnp.float32)
                im = im + rbuf[j, 1, rows, :].astype(jnp.float32)
                if folded:
                    re = re + held[0, rows, :]
                    im = im + held[1, rows, :]
                re, im = -re, -im
            re = re.astype(obuf.dtype)
            im = im.astype(obuf.dtype)
            obuf[j, 0, rows, :] = re
            obuf[j, 1, rows, :] = im
            out_copy(r, j).start()
        if last:
            total = weight[pole, 0] * im.astype(jnp.float32) + weight[pole, 1] * re.astype(jnp.float32)
            total = total + (base[rows, :] if folded else other_poles(rows))
            d32[rows, :] = total
            d16[rows, :] = total.astype(jnp.bfloat16)
        if fold:
            sbuf[rows, :] = other_poles(rows)
            sum_copy(r).start()
        return carry

    lax.fori_loop(0, row_tiles, step, 0)

    if last:
        share = d32.shape[0] // n_pole
        mine = meta[2 * row_tiles]
        copies = []
        for d in range(n_pole):
            block = lax.rem(mine + d, n_pole)
            rows = pl.ds(pl.multiple_of(block * share, share), share)
            copies.append(
                pltpu.make_async_copy((d16 if d else d32).at[rows, :], dens[d], dsem.at[d])
            )
        for copy in copies:
            copy.start()
        for copy in copies:
            copy.wait()

    def drain(r, carry):
        for j in range(n_parts):
            out_copy(r, j).wait()
        if fold:
            sum_copy(r).wait()
        return carry

    lax.fori_loop(0, row_tiles, drain, 0)


def slice_product(cfg, meta, weight, inverse, arrays, width, recv=None, panel=None, earlier=()):
    poles, _, rows, _ = inverse.shape
    tile, row_tiles, n_pole, parts = cfg["tile"], cfg["row_tiles"], cfg["n_pole"], cfg["parts"]
    keep, fold, last = cfg["kind"] == "keep", cfg["kind"] == "fold", cfg["last"]
    n_buf = min(row_tiles, 4)
    depth = cfg["span"][1] * tile
    n_parts = len(parts)
    names = sorted({name for part, _ in parts for name in part})
    part_shape = (2, rows, width)
    operands = [meta, weight, inverse, *(arrays[name] for name in names)]
    specs = [SMEM, SMEM] + [ANY] * (1 + len(names))
    aliases = {}
    outs = []
    if keep:
        operands += [*recv, *earlier]
        specs += [ANY] * (n_parts + len(earlier))
        outs.append(jax.ShapeDtypeStruct((poles, 2, rows, cfg["panel_width"]), jnp.bfloat16))
        if panel is not None:
            aliases = {len(operands): 0}
            operands.append(panel)
            specs.append(ANY)
    elif fold:
        operands.append(panel)
        specs.append(ANY)
        outs += [jax.ShapeDtypeStruct(part_shape, jnp.float32), jax.ShapeDtypeStruct((rows, width), jnp.float32)]
    else:
        outs += [jax.ShapeDtypeStruct(part_shape, jnp.bfloat16)] * n_parts
    if last:
        share = rows // n_pole
        for d in range(n_pole):
            outs.append(jax.ShapeDtypeStruct((share, width), jnp.bfloat16 if d else jnp.float32))
    scratch = [
        pltpu.VMEM((n_buf, 2, tile, depth), jnp.bfloat16),
        pltpu.VMEM((depth, 2 * width * n_parts), jnp.bfloat16),
        pltpu.VMEM((2 * tile, 2 * width * n_parts), jnp.float32),
        pltpu.VMEM((n_parts, *part_shape), jnp.float32 if fold else jnp.bfloat16),
        pltpu.SemaphoreType.DMA((n_buf, 2)),
        pltpu.SemaphoreType.DMA((n_parts, 2)),
        pltpu.SemaphoreType.DMA((row_tiles, n_parts)),
    ]
    if keep:
        scratch += [pltpu.VMEM((n_parts, *part_shape), jnp.bfloat16), pltpu.SemaphoreType.DMA((n_parts,))]
    if fold or (last and not earlier):
        scratch += [
            pltpu.VMEM((max(poles - 1, 1), *part_shape), jnp.bfloat16),
            pltpu.SemaphoreType.DMA((max(poles - 1, 1),)),
        ]
    if last and earlier:
        scratch += [pltpu.VMEM(part_shape, jnp.float32), pltpu.SemaphoreType.DMA]
        scratch += [pltpu.VMEM((rows, width), jnp.float32), pltpu.SemaphoreType.DMA]
    if last:
        scratch += [
            pltpu.VMEM((rows, width), jnp.float32),
            pltpu.VMEM((rows, width), jnp.bfloat16),
            pltpu.SemaphoreType.DMA((n_pole,)),
        ]
    if fold:
        scratch += [pltpu.VMEM((rows, width), jnp.float32), pltpu.SemaphoreType.DMA((row_tiles,))]
    cfg = dict(cfg, aliased=len(aliases), arrays=names)
    return pl.pallas_call(
        functools.partial(slice_kernel, cfg),
        out_shape=outs,
        in_specs=specs,
        out_specs=[ANY] * len(outs),
        scratch_shapes=scratch,
        input_output_aliases=aliases,
        compiler_params=pltpu.CompilerParams(vmem_limit_bytes=30 * 2**20),
        cost_estimate=pl.CostEstimate(flops=300 * rows * depth * n_parts, bytes_accessed=rows * width, transcendentals=0),
        name=cfg["name"],
    )(*operands)


def half_order(n_col, half, z):
    group = n_col // 2
    return sorted(range(half * group, (half + 1) * group), key=lambda s: abs(s - z))


def plan_transfers(n_col, poles):
    end, half = poles - 1, n_col // 2
    where = {(z, y, p, z): ("own", p) for z in range(n_col) for y in range(2) for p in range(poles)}
    lists = {"out": [], "across": [], "in": []}
    at = {}

    def add(kind, name, moves):
        moves = [m for m in moves if m[3] < n_col and m[4] < n_col]
        if not moves:
            return
        both = moves + [
            (n_col - 1 - z, n_col - 1 - to, p, n_col - 1 - s1, n_col - 1 - s0) for z, to, p, s0, s1 in moves
        ]
        for z, to, p, s0, s1 in both:
            where[(to, 0, p, s0)] = where[(to, 1, p, s1)] = name
        at[name] = len(lists[kind])
        lists[kind].append((name, both))

    def hop(z, p, step):
        return (z, z - 1, p, z + step - 1, z + step - 1)

    steps = range(1, n_col)
    pairs = [(p, step) for p in range(end) for step in steps]
    pairs = sorted(pairs, key=lambda item: (item[0] * (n_col - 1) + item[1] - 3 * (item[1] == 1), item))

    def add_end(i):
        far = [hop(z, end, i + 1) for z in range(2, half)]
        add("out", f"o{end}s{i + 1}", [(1, 0, end, first_row[i], second_row[i])] + [m for m in far if m[3] < n_col])

    first_row = sorted(steps, key=lambda s: (s < half, s))
    second_row = sorted(steps, key=lambda s: (s != half, s))
    for p, step in pairs[:-1]:
        add("out", f"o{p}s{step}", [hop(z, p, step) for z in range(1, half)])
    add_end(0)
    for p, step in pairs[-1:]:
        add("out", f"o{p}s{step}", [hop(z, p, step) for z in range(1, half)])
    for i in range(1, len(first_row)):
        add_end(i)
    pairs = [(p, step) for p in range(poles) for step in range(1, half + 1)]
    pairs = sorted(pairs, key=lambda item: (item[0] - (item == (end, 1)), item == (end - 1, half), item))
    for p, step in pairs:
        add("across", f"a{p}s{step}", [hop(half, p, step)])
    for p in range(poles):
        for step in steps:
            add("in", f"i{p}s{step}", [hop(z, p, step) for z in range(half + 1, n_col)])
    return lists, where, at


def make_fast_body(n_col, n_pole, tile):
    group = n_col // 2
    places = [(zz, yy) for zz in range(n_col) for yy in range(2)]

    def body(inverse, lower, mask_tiles, pole_weight):
        poles, _, rows, depth = inverse.shape
        width = lower.shape[3]
        row_tiles, col_tiles = rows // tile, depth // tile
        end = poles - 1
        z, y, mine = lax.axis_index("col"), lax.axis_index("row"), lax.axis_index("pole")
        lists, where, ready = plan_transfers(n_col, poles)
        final = len(lists["out"]) - 1
        final_name = lists["out"][final][0]
        cuts = col_tiles - max(1, 3 * col_tiles // 8) if col_tiles > 1 and poles > 1 else 0

        head_size = 2 * row_tiles + 1
        tables = []
        calls = []
        for p in range(poles):
            for kind in ("send", "keep"):
                for bunch in [[i] for i in range(group)]:
                    parts = []
                    for i in bunch:
                        names, picks, columns = [], np.zeros((n_col, 2), np.int32), np.zeros((n_col, 2), np.int32)
                        for zz, yy in places:
                            half = yy if kind == "keep" else 1 - yy
                            s = half_order(n_col, half, zz)[i]
                            name = where[(zz, yy, p, s)]
                            name = "own" if isinstance(name, tuple) else name
                            if name not in names:
                                names.append(name)
                            picks[zz, yy] = names.index(name)
                            columns[zz, yy] = s - half * group
                        parts.append((names, head_size + len(tables)))
                        tables += [picks, columns]
                    calls.append((p, kind, tuple(bunch), parts))
        chosen = lax.dynamic_slice(jnp.asarray(np.stack(tables)), (0, z, y), (len(tables), 1, 1)).reshape(-1)

        own = lax.dynamic_slice(mask_tiles, (z * row_tiles, y * col_tiles), (row_tiles, col_tiles))
        count = jnp.sum(own, axis=1)
        modes = jnp.where(count == col_tiles, FULL, jnp.where(count == 0, 0, SINGLE))
        single = jnp.argmax(own, axis=1)
        meta = jnp.concatenate([modes, single, jnp.reshape(mine, (1,)), chosen]).astype(jnp.int32)

        arrays = {"own": lower}
        rest = lower
        for p in range(poles):
            arrays[("own", p)] = rest[p]
            rest, arrays[("own", p)] = lax.optimization_barrier((rest, arrays[("own", p)]))

        queue = [[] for _ in range(final + 1)]
        sent_at = {}
        for call in calls:
            p, kind, bunch, parts = call
            t = max([ready.get(name, 0) for names, _ in parts for name in names])
            if kind == "send":
                sent_at.update({(p, i): t for i in bunch})
            else:
                t = min(max([t] + [sent_at[(p, i)] + 1 for i in bunch]), final)
            queue[t].append(call)

        late = {"meta": meta}
        state = {"panel": None, "part": {}, "sent": {}, "dens": {}}

        def run(call):
            p, kind, bunch, parts = call
            cfg = dict(
                name=f"{kind}_{p}_{bunch[0]}",
                kind=kind,
                last=kind == "keep" and p == end,
                parts=parts,
                pole=p,
                tile=tile,
                row_tiles=row_tiles,
                n_pole=n_pole,
                panel_width=group * width,
                span=(0, col_tiles),
                cut=[],
            )
            if kind == "send":
                made = slice_product(cfg, late["meta"], pole_weight, inverse, arrays, width)
                for i, part in zip(bunch, made):
                    state["part"][(p, i)] = part
                    state["sent"][(p, i)] = lax.ppermute(part, "row", [(0, 1), (1, 0)])
                return
            recv = [state["sent"][(p, i)] for i in bunch]
            sources, earlier = arrays, ()
            if cuts and final_name in parts[0][0]:
                sources = dict(arrays, **{final_name: arrays[final_name][0]})
                first = dict(cfg, name=f"fold_{p}_{bunch[0]}", kind="fold", last=False, span=(0, cuts), cut=[final_name])
                earlier = slice_product(
                    first, late["meta"], pole_weight, inverse, sources, width, panel=state["panel"]
                )
                sources = dict(arrays, **{final_name: arrays[final_name][1]})
                cfg.update(span=(cuts, col_tiles - cuts), cut=[final_name])
            panel, *shares = slice_product(
                cfg, late["meta"], pole_weight, inverse, sources, width, recv, state["panel"], earlier
            )
            state["panel"] = panel
            if shares:
                total = shares[0]
                for d in range(1, n_pole):
                    ways = [(q, (q + d) % n_pole) for q in range(n_pole)]
                    total = total + lax.ppermute(shares[d], "pole", ways).astype(jnp.float32)
                state["dens"][bunch[0]] = total

        def is_one_of(spots):
            return functools.reduce(jnp.logical_or, [(z == a) & (y == b) for a, b in spots])

        def launch(kind, t, deps):
            if t >= len(lists[kind]):
                return
            name, moves = lists[kind][t]
            held = {}
            for zz, _, p, s0, s1 in moves:
                for yy, s in ((0, s0), (1, s1)):
                    held.setdefault(where[(zz, yy, p, s)], []).append((zz, yy))
            held = sorted(held.items(), key=lambda item: -len(item[1]))
            values = [arrays[source] for source, _ in held]
            values, state["panel"], _ = lax.optimization_barrier((values, state["panel"], deps))
            ways = [(zz, to) for zz, to, *_ in moves]
            pieces = [slice(None)]
            if name == final_name and cuts:
                pieces = [slice(0, cuts * tile), slice(cuts * tile, None)]
            moved = []
            for piece in pieces:
                value = values[0][:, piece]
                for other, (_, spots) in zip(values[1:], held[1:]):
                    value = jnp.where(is_one_of(spots), other[:, piece], value)
                moved.append(lax.ppermute(value, "col", ways))
            arrays[name] = moved if len(moved) > 1 else moved[0]

        def landed(kind, t):
            return [arrays[lists[kind][t][0]]] if 0 <= t < len(lists[kind]) else []

        launch("out", 0, [])
        launch("across", 0, [])
        launch("in", 0, [])
        launch("out", 1, [])
        launch("across", 1, [])
        for t in range(final + 1):
            deps = landed("out", t)
            deps += [state["part"][key] for key, at in sent_at.items() if at == t - 1]
            deps += [state["sent"][key] for key, at in sent_at.items() if at == t - 2]
            launch("out", t + 2, deps)
            launch("across", t + 2, landed("out", t) + landed("across", t))
            launch("in", t + 1, landed("out", t) + landed("in", t))
            for kind in ("send", "keep"):
                for call in queue[t]:
                    if call[1] == kind:
                        run(call)
                if t >= final - 2:
                    made = [state["part"][key] for key, at in sent_at.items() if at == t]
                    late["meta"], state["panel"], _ = lax.optimization_barrier((late["meta"], state["panel"], made))

        columns = []
        for c in range(group):
            value = state["dens"][0]
            for i in range(1, group):
                spots = [(a, b) for a, b in places if half_order(n_col, b, a)[i] - b * group == c]
                value = jnp.where(is_one_of(spots), state["dens"][i], value)
            columns.append(value)
        return (state["panel"], jnp.concatenate(columns, axis=1))

    return body


def solution(mesh):
    n_pole, n_row, n_col = (mesh.shape[name] for name in ("pole", "row", "col"))

    def whole(inverse, lower, mask_tiles, pole_weight):
        tile = inverse.shape[2] // mask_tiles.shape[0]
        width = lower.shape[3] // n_col
        rows = inverse.shape[2] // n_col
        fits = n_row == 2 and n_col % 2 == 0 and n_col > 2 and width % LANES == 0
        fits = fits and tile % LANES == 0 and rows % (16 * n_pole) == 0 and inverse.shape[0] > n_pole
        if fits:
            body = make_fast_body(n_col, n_pole, tile)
        else:
            body = functools.partial(general_body, tile)
        return jax.shard_map(
            body,
            mesh=mesh,
            in_specs=(
                P("pole", None, "col", "row"),
                P("pole", None, "row", "col"),
                P(),
                P("pole", None),
            ),
            out_specs=(P("pole", None, "col", "row"), P(("col", "pole"), "row")),
            check_vma=False,
        )(inverse, lower, mask_tiles, pole_weight)

    return whole
```

```python
import functools

import jax
import jax.numpy as jnp
import numpy as np
from jax import lax
from jax.experimental import pallas as pl
from jax.experimental.pallas import tpu as pltpu
from jax.sharding import PartitionSpec as P

ANY = pl.BlockSpec(memory_space=pl.ANY)
SMEM = pl.BlockSpec(memory_space=pltpu.SMEM)
LANES = 128
FULL, SINGLE = 2, 1


def complex_product(block, factors):
    real_part = jnp.einsum(
        "prc,pcw->prw", block[:, 0], factors[:, 0], preferred_element_type=jnp.float32
    ) - jnp.einsum("prc,pcw->prw", block[:, 1], factors[:, 1], preferred_element_type=jnp.float32)
    imag_part = jnp.einsum(
        "prc,pcw->prw", block[:, 0], factors[:, 1], preferred_element_type=jnp.float32
    ) + jnp.einsum("prc,pcw->prw", block[:, 1], factors[:, 0], preferred_element_type=jnp.float32)
    return jnp.stack([real_part, imag_part], axis=1)


def general_body(tile, inverse, lower, mask_tiles, pole_weight):
    full_lower = lax.all_gather(lower, "col", axis=3, tiled=True)
    row_tiles = inverse.shape[2] // tile
    col_tiles = inverse.shape[3] // tile
    start = (lax.axis_index("col") * row_tiles, lax.axis_index("row") * col_tiles)
    own = lax.dynamic_slice(mask_tiles, start, (row_tiles, col_tiles))
    keep = jnp.repeat(jnp.repeat(own, tile, axis=0), tile, axis=1).astype(inverse.dtype)
    partial_value = complex_product(inverse * keep[None, None], full_lower)
    summed = lax.psum_scatter(
        partial_value.astype(jnp.bfloat16), "row", scatter_dimension=3, tiled=True
    ).astype(jnp.float32)
    panel = (-summed).astype(jnp.bfloat16)
    values = panel.astype(jnp.float32)
    weighted = jnp.sum(
        pole_weight[:, 0, None, None] * values[:, 1] + pole_weight[:, 1, None, None] * values[:, 0],
        axis=0,
    )
    density = lax.psum_scatter(
        weighted.astype(jnp.bfloat16), "pole", scatter_dimension=0, tiled=True
    ).astype(jnp.float32)
    return (panel, density)


def slice_kernel(cfg, *refs):
    pole, tile, row_tiles, n_pole = (cfg[k] for k in ("pole", "tile", "row_tiles", "n_pole"))
    parts = cfg["parts"]
    n_parts = len(parts)
    keep, fold, last = cfg["kind"] == "keep", cfg["kind"] == "fold", cfg["last"]
    low_tile, n_tiles = cfg["span"]
    folded = low_tile > 0
    span = pl.ds(low_tile * tile, n_tiles * tile)
    refs = list(refs)

    def take(count):
        taken = refs[:count]
        del refs[:count]
        return taken

    meta, weight, inv = take(3)
    cands = dict(zip(cfg["arrays"], take(len(cfg["arrays"]))))
    if keep:
        recv = take(n_parts)
        earlier = take(2 if folded else 0)
        take(cfg["aliased"])
    if fold:
        (panel,) = take(1)
    outs = take(2 if fold else 1 if keep else n_parts)
    if keep:
        (panel,) = outs
    dens = take(n_pole if last else 0)
    abuf, wbuf, prod, obuf, asem, wsem, osem = take(7)
    width = wbuf.shape[1] // (2 * n_parts)
    depth = wbuf.shape[0]
    n_buf = abuf.shape[0]

    def start(copy):
        copy.start()

    def wait(copy):
        copy.wait()

    def tile_rows(r):
        return pl.ds(pl.multiple_of(r * tile, tile), tile)

    def single(r):
        at = meta[row_tiles + r]
        return (meta[r] == SINGLE) & (at >= low_tile) & (at < low_tile + n_tiles)

    def fetch(r, act):
        slot = lax.rem(r, n_buf)

        @pl.when(meta[r] == FULL)
        def _():
            for c in range(2):
                act(pltpu.make_async_copy(inv.at[pole, c, tile_rows(r), span], abuf.at[slot, c], asem.at[slot, c]))

        @pl.when(single(r))
        def _():
            cols = tile_rows(meta[row_tiles + r])
            for c in range(2):
                act(
                    pltpu.make_async_copy(
                        inv.at[pole, c, tile_rows(r), cols], abuf.at[slot, c, :, pl.ds(0, tile)], asem.at[slot, c]
                    )
                )

    def lower_copies(j, ref):
        return [
            pltpu.make_async_copy(ref[h], wbuf.at[:, pl.ds((2 * j + h) * width, width)], wsem.at[j, h])
            for h in range(2)
        ]

    def source(name):
        whole = cands[name].at[pole] if name == "own" else cands[name]
        return [whole.at[h] if name in cfg["cut"] else whole.at[h, span, :] for h in range(2)]

    for j, (names, base) in enumerate(parts):
        for i, name in enumerate(names):

            @pl.when(meta[base] == i)
            def _(j=j, name=name):
                for copy in lower_copies(j, source(name)):
                    copy.start()

    fetch(0, start)
    columns = [pl.ds(pl.multiple_of(meta[base + 1] * width, width), width) for _, base in parts]
    extras = []
    if keep:
        rbuf, rsem = take(2)
        extras += [pltpu.make_async_copy(recv[j], rbuf.at[j], rsem.at[j]) for j in range(n_parts)]
    if fold or (last and not folded):
        pbuf, psem = take(2)
        extras += [
            pltpu.make_async_copy(panel.at[q, :, :, columns[0]], pbuf.at[q], psem.at[q]) for q in range(pole)
        ]
    if last and folded:
        held, hsem = take(2)
        base, bsem = take(2)
        extras += [pltpu.make_async_copy(earlier[0], held, hsem), pltpu.make_async_copy(earlier[1], base, bsem)]
    if last:
        d32, d16, dsem = take(3)
    for copy in extras:
        copy.start()
    for r in range(1, min(n_buf, row_tiles)):
        fetch(r, start)
    for j, (names, _) in enumerate(parts):
        for copy in lower_copies(j, source(names[0])):
            copy.wait()

    def out_copy(r, j):
        rows = tile_rows(r)
        target = panel.at[pole, :, rows, columns[j]] if keep else outs[j].at[:, rows, :]
        return pltpu.make_async_copy(obuf.at[j, :, rows, :], target, osem.at[r, j])

    def sum_copy(r):
        return pltpu.make_async_copy(sbuf.at[tile_rows(r), :], outs[1].at[tile_rows(r), :], ssem.at[r])

    def other_poles(rows):
        return sum(
            weight[q, 0] * pbuf[q, 1, rows, :].astype(jnp.float32)
            + weight[q, 1] * pbuf[q, 0, rows, :].astype(jnp.float32)
            for q in range(pole)
        )

    if fold:
        sbuf, ssem = take(2)

    def step(r, carry):
        slot = lax.rem(r, n_buf)
        rows = tile_rows(r)
        fetch(r, wait)

        @pl.when(meta[r] == FULL)
        def _():
            both = abuf[slot].reshape(2 * tile, n_tiles * tile)
            prod[...] = jnp.dot(both, wbuf[...], preferred_element_type=jnp.float32)

        @pl.when(single(r))
        def _():
            both = abuf[slot, :, :, :tile].reshape(2 * tile, tile)
            prod[...] = jnp.dot(both, wbuf[tile_rows(meta[row_tiles + r] - low_tile), :], preferred_element_type=jnp.float32)

        @pl.when((meta[r] != FULL) & jnp.logical_not(single(r)))
        def _():
            prod[...] = jnp.zeros_like(prod)

        if extras:

            @pl.when(r == 0)
            def _():
                for copy in extras:
                    copy.wait()

        if row_tiles > n_buf:

            @pl.when(r + n_buf < row_tiles)
            def _():
                fetch(r + n_buf, start)

        for j in range(n_parts):
            low, high = (pl.ds((2 * j + h) * width, width) for h in range(2))
            re = prod[:tile, low] - prod[tile:, high]
            im = prod[:tile, high] + prod[tile:, low]
            if keep:
                re = re + rbuf[j, 0, rows, :].astype(jnp.float32)
                im = im + rbuf[j, 1, rows, :].astype(jnp.float32)
                if folded:
                    re = re + held[0, rows, :]
                    im = im + held[1, rows, :]
                re, im = -re, -im
            re = re.astype(obuf.dtype)
            im = im.astype(obuf.dtype)
            obuf[j, 0, rows, :] = re
            obuf[j, 1, rows, :] = im
            out_copy(r, j).start()
        if last:
            total = weight[pole, 0] * im.astype(jnp.float32) + weight[pole, 1] * re.astype(jnp.float32)
            total = total + (base[rows, :] if folded else other_poles(rows))
            d32[rows, :] = total
            d16[rows, :] = total.astype(jnp.bfloat16)
        if fold:
            sbuf[rows, :] = other_poles(rows)
            sum_copy(r).start()
        return carry

    lax.fori_loop(0, row_tiles, step, 0)

    if last:
        share = d32.shape[0] // n_pole
        mine = meta[2 * row_tiles]
        copies = []
        for d in range(n_pole):
            block = lax.rem(mine + d, n_pole)
            rows = pl.ds(pl.multiple_of(block * share, share), share)
            copies.append(
                pltpu.make_async_copy((d16 if d else d32).at[rows, :], dens[d], dsem.at[d])
            )
        for copy in copies:
            copy.start()
        for copy in copies:
            copy.wait()

    def drain(r, carry):
        for j in range(n_parts):
            out_copy(r, j).wait()
        if fold:
            sum_copy(r).wait()
        return carry

    lax.fori_loop(0, row_tiles, drain, 0)


def slice_product(cfg, meta, weight, inverse, arrays, width, recv=None, panel=None, earlier=()):
    poles, _, rows, _ = inverse.shape
    tile, row_tiles, n_pole, parts = cfg["tile"], cfg["row_tiles"], cfg["n_pole"], cfg["parts"]
    keep, fold, last = cfg["kind"] == "keep", cfg["kind"] == "fold", cfg["last"]
    n_buf = min(row_tiles, 4)
    depth = cfg["span"][1] * tile
    n_parts = len(parts)
    names = sorted({name for part, _ in parts for name in part})
    part_shape = (2, rows, width)
    operands = [meta, weight, inverse, *(arrays[name] for name in names)]
    specs = [SMEM, SMEM] + [ANY] * (1 + len(names))
    aliases = {}
    outs = []
    if keep:
        operands += [*recv, *earlier]
        specs += [ANY] * (n_parts + len(earlier))
        outs.append(jax.ShapeDtypeStruct((poles, 2, rows, cfg["panel_width"]), jnp.bfloat16))
        if panel is not None:
            aliases = {len(operands): 0}
            operands.append(panel)
            specs.append(ANY)
    elif fold:
        operands.append(panel)
        specs.append(ANY)
        outs += [jax.ShapeDtypeStruct(part_shape, jnp.float32), jax.ShapeDtypeStruct((rows, width), jnp.float32)]
    else:
        outs += [jax.ShapeDtypeStruct(part_shape, jnp.bfloat16)] * n_parts
    if last:
        share = rows // n_pole
        for d in range(n_pole):
            outs.append(jax.ShapeDtypeStruct((share, width), jnp.bfloat16 if d else jnp.float32))
    scratch = [
        pltpu.VMEM((n_buf, 2, tile, depth), jnp.bfloat16),
        pltpu.VMEM((depth, 2 * width * n_parts), jnp.bfloat16),
        pltpu.VMEM((2 * tile, 2 * width * n_parts), jnp.float32),
        pltpu.VMEM((n_parts, *part_shape), jnp.float32 if fold else jnp.bfloat16),
        pltpu.SemaphoreType.DMA((n_buf, 2)),
        pltpu.SemaphoreType.DMA((n_parts, 2)),
        pltpu.SemaphoreType.DMA((row_tiles, n_parts)),
    ]
    if keep:
        scratch += [pltpu.VMEM((n_parts, *part_shape), jnp.bfloat16), pltpu.SemaphoreType.DMA((n_parts,))]
    if fold or (last and not earlier):
        scratch += [
            pltpu.VMEM((max(poles - 1, 1), *part_shape), jnp.bfloat16),
            pltpu.SemaphoreType.DMA((max(poles - 1, 1),)),
        ]
    if last and earlier:
        scratch += [pltpu.VMEM(part_shape, jnp.float32), pltpu.SemaphoreType.DMA]
        scratch += [pltpu.VMEM((rows, width), jnp.float32), pltpu.SemaphoreType.DMA]
    if last:
        scratch += [
            pltpu.VMEM((rows, width), jnp.float32),
            pltpu.VMEM((rows, width), jnp.bfloat16),
            pltpu.SemaphoreType.DMA((n_pole,)),
        ]
    if fold:
        scratch += [pltpu.VMEM((rows, width), jnp.float32), pltpu.SemaphoreType.DMA((row_tiles,))]
    cfg = dict(cfg, aliased=len(aliases), arrays=names)
    return pl.pallas_call(
        functools.partial(slice_kernel, cfg),
        out_shape=outs,
        in_specs=specs,
        out_specs=[ANY] * len(outs),
        scratch_shapes=scratch,
        input_output_aliases=aliases,
        compiler_params=pltpu.CompilerParams(vmem_limit_bytes=48 * 2**20),
        cost_estimate=pl.CostEstimate(flops=30 * rows * depth * n_parts, bytes_accessed=rows * width, transcendentals=0),
        name=cfg["name"],
    )(*operands)


def half_order(n_col, half, z):
    group = n_col // 2
    return sorted(range(half * group, (half + 1) * group), key=lambda s: abs(s - z))


def plan_transfers(n_col, poles):
    end, half = poles - 1, n_col // 2
    where = {(z, y, p, z): ("own", p) for z in range(n_col) for y in range(2) for p in range(poles)}
    lists = {"out": [], "across": [], "in": []}
    at = {}

    def add(kind, name, moves):
        moves = [m for m in moves if m[3] < n_col and m[4] < n_col]
        if not moves:
            return
        both = moves + [
            (n_col - 1 - z, n_col - 1 - to, p, n_col - 1 - s1, n_col - 1 - s0) for z, to, p, s0, s1 in moves
        ]
        for z, to, p, s0, s1 in both:
            where[(to, 0, p, s0)] = where[(to, 1, p, s1)] = name
        at[name] = len(lists[kind])
        lists[kind].append((name, both))

    def hop(z, p, step):
        return (z, z - 1, p, z + step - 1, z + step - 1)

    steps = range(1, n_col)
    pairs = [(p, step) for p in range(end) for step in steps]
    pairs = sorted(pairs, key=lambda item: (item[0] * (n_col - 1) + item[1] - 3 * (item[1] == 1), item))

    def add_end(i):
        far = [hop(z, end, i + 1) for z in range(2, half)]
        add("out", f"o{end}s{i + 1}", [(1, 0, end, first_row[i], second_row[i])] + [m for m in far if m[3] < n_col])

    first_row = sorted(steps, key=lambda s: (s < half, s))
    second_row = sorted(steps, key=lambda s: (s != half, s))
    def add_out(p, step):
        moves = [hop(z, p, step) for z in range(1, half)]
        inwards = [hop(z, p, step) for z in range(half + 1, n_col)]
        if step == 1 and half == 2:
            moves += inwards
            joined.add(p)
        add("out", f"o{p}s{step}", moves)

    joined = set()
    for p, step in pairs[:-1]:
        add_out(p, step)
    add_end(0)
    for p, step in pairs[-1:]:
        add_out(p, step)
    for i in range(1, len(first_row)):
        add_end(i)
    pairs = [(p, step) for p in range(poles) for step in range(1, half + 1)]
    pairs = sorted(pairs, key=lambda item: (item[0] - (item == (end, 1)), item == (end - 1, half), item))
    for p, step in pairs:
        add("across", f"a{p}s{step}", [hop(half, p, step)])
    for p in range(poles):
        for step in steps:
            if step > 1 or p not in joined:
                add("in", f"i{p}s{step}", [hop(z, p, step) for z in range(half + 1, n_col)])
    return lists, where, at


def make_fast_body(n_col, n_pole, tile):
    group = n_col // 2
    places = [(zz, yy) for zz in range(n_col) for yy in range(2)]

    def body(inverse, lower, mask_tiles, pole_weight):
        poles, _, rows, depth = inverse.shape
        width = lower.shape[3]
        row_tiles, col_tiles = rows // tile, depth // tile
        end = poles - 1
        z, y, mine = lax.axis_index("col"), lax.axis_index("row"), lax.axis_index("pole")
        lists, where, ready = plan_transfers(n_col, poles)
        final = len(lists["out"]) - 1
        final_name = lists["out"][final][0]
        cuts = col_tiles - max(1, 3 * col_tiles // 8) if col_tiles > 1 and poles > 1 else 0

        head_size = 2 * row_tiles + 1
        tables = []
        calls = []
        for p in range(poles):
            for kind in ("send", "keep"):
                for bunch in [[i] for i in range(group)]:
                    parts = []
                    for i in bunch:
                        names, picks, columns = [], np.zeros((n_col, 2), np.int32), np.zeros((n_col, 2), np.int32)
                        for zz, yy in places:
                            half = yy if kind == "keep" else 1 - yy
                            s = half_order(n_col, half, zz)[i]
                            name = where[(zz, yy, p, s)]
                            name = "own" if isinstance(name, tuple) else name
                            if name not in names:
                                names.append(name)
                            picks[zz, yy] = names.index(name)
                            columns[zz, yy] = s - half * group
                        parts.append((names, head_size + len(tables)))
                        tables += [picks, columns]
                    calls.append((p, kind, tuple(bunch), parts))
        chosen = lax.dynamic_slice(jnp.asarray(np.stack(tables)), (0, z, y), (len(tables), 1, 1)).reshape(-1)

        own = lax.dynamic_slice(mask_tiles, (z * row_tiles, y * col_tiles), (row_tiles, col_tiles))
        count = jnp.sum(own, axis=1)
        modes = jnp.where(count == col_tiles, FULL, jnp.where(count == 0, 0, SINGLE))
        single = jnp.argmax(own, axis=1)
        meta = jnp.concatenate([modes, single, jnp.reshape(mine, (1,)), chosen]).astype(jnp.int32)

        arrays = {"own": lower}
        rest = lower
        for p in range(poles):
            arrays[("own", p)] = rest[p]
            rest, arrays[("own", p)] = lax.optimization_barrier((rest, arrays[("own", p)]))

        queue = [[] for _ in range(final + 1)]
        sent_at = {}
        for call in calls:
            p, kind, bunch, parts = call
            t = max([ready.get(name, 0) for names, _ in parts for name in names])
            if kind == "send":
                sent_at.update({(p, i): t for i in bunch})
            else:
                t = min(max([t] + [sent_at[(p, i)] + 1 for i in bunch]), final)
            queue[t].append(call)

        late = {"meta": meta}
        state = {"panel": None, "part": {}, "sent": {}, "dens": {}}

        def run(call):
            p, kind, bunch, parts = call
            cfg = dict(
                name=f"{kind}_{p}_{bunch[0]}",
                kind=kind,
                last=kind == "keep" and p == end,
                parts=parts,
                pole=p,
                tile=tile,
                row_tiles=row_tiles,
                n_pole=n_pole,
                panel_width=group * width,
                span=(0, col_tiles),
                cut=[],
            )
            if kind == "send":
                made = slice_product(cfg, late["meta"], pole_weight, inverse, arrays, width)
                for i, part in zip(bunch, made):
                    state["part"][(p, i)] = part
                    state["sent"][(p, i)] = lax.ppermute(part, "row", [(0, 1), (1, 0)])
                return
            recv = [state["sent"][(p, i)] for i in bunch]
            sources, earlier = arrays, ()
            if cuts and final_name in parts[0][0]:
                sources = dict(arrays, **{final_name: arrays[final_name][0]})
                first = dict(cfg, name=f"fold_{p}_{bunch[0]}", kind="fold", last=False, span=(0, cuts), cut=[final_name])
                earlier = slice_product(
                    first, late["meta"], pole_weight, inverse, sources, width, panel=state["panel"]
                )
                sources = dict(arrays, **{final_name: arrays[final_name][1]})
                cfg.update(span=(cuts, col_tiles - cuts), cut=[final_name])
            panel, *shares = slice_product(
                cfg, late["meta"], pole_weight, inverse, sources, width, recv, state["panel"], earlier
            )
            state["panel"] = panel
            if shares:
                total = shares[0]
                for d in range(1, n_pole):
                    ways = [(q, (q + d) % n_pole) for q in range(n_pole)]
                    total = total + lax.ppermute(shares[d], "pole", ways).astype(jnp.float32)
                state["dens"][bunch[0]] = total

        def is_one_of(spots):
            return functools.reduce(jnp.logical_or, [(z == a) & (y == b) for a, b in spots])

        def launch(kind, t, deps):
            if t >= len(lists[kind]):
                return
            name, moves = lists[kind][t]
            held = {}
            for zz, _, p, s0, s1 in moves:
                for yy, s in ((0, s0), (1, s1)):
                    held.setdefault(where[(zz, yy, p, s)], []).append((zz, yy))
            held = sorted(held.items(), key=lambda item: -len(item[1]))
            values = [arrays[source] for source, _ in held]
            values, state["panel"], _ = lax.optimization_barrier((values, state["panel"], deps))
            ways = [(zz, to) for zz, to, *_ in moves]
            pieces = [slice(None)]
            if name == final_name and cuts:
                pieces = [slice(0, cuts * tile), slice(cuts * tile, None)]
            moved = []
            for piece in pieces:
                value = values[0][:, piece]
                for other, (_, spots) in zip(values[1:], held[1:]):
                    value = jnp.where(is_one_of(spots), other[:, piece], value)
                moved.append(lax.ppermute(value, "col", ways))
            arrays[name] = moved if len(moved) > 1 else moved[0]

        def landed(kind, t):
            return [arrays[lists[kind][t][0]]] if 0 <= t < len(lists[kind]) else []

        launch("out", 0, [])
        launch("across", 0, [])
        launch("out", 1, [])
        launch("across", 1, [])
        for t in range(final + 1):
            deps = landed("out", t)
            deps += [state["part"][key] for key, at in sent_at.items() if at == t - 1]
            deps += [state["sent"][key] for key, at in sent_at.items() if at == t - 2]
            launch("out", t + 2, deps)
            launch("across", t + 2, landed("out", t) + landed("across", t))
            launch("in", t, landed("out", t) + landed("in", t - 1))
            for kind in ("send", "keep"):
                for call in queue[t]:
                    if call[1] == kind:
                        run(call)
                if t >= final - 2:
                    made = [state["part"][key] for key, at in sent_at.items() if at == t]
                    late["meta"], state["panel"], _ = lax.optimization_barrier((late["meta"], state["panel"], made))

        columns = []
        for c in range(group):
            value = state["dens"][0]
            for i in range(1, group):
                spots = [(a, b) for a, b in places if half_order(n_col, b, a)[i] - b * group == c]
                value = jnp.where(is_one_of(spots), state["dens"][i], value)
            columns.append(value)
        return (state["panel"], jnp.concatenate(columns, axis=1))

    return body


def solution(mesh):
    n_pole, n_row, n_col = (mesh.shape[name] for name in ("pole", "row", "col"))

    def whole(inverse, lower, mask_tiles, pole_weight):
        tile = inverse.shape[2] // mask_tiles.shape[0]
        width = lower.shape[3] // n_col
        rows = inverse.shape[2] // n_col
        fits = n_row == 2 and n_col % 2 == 0 and n_col > 2 and width % LANES == 0
        fits = fits and tile % LANES == 0 and rows % (16 * n_pole) == 0 and inverse.shape[0] > n_pole
        if fits:
            body = make_fast_body(n_col, n_pole, tile)
        else:
            body = functools.partial(general_body, tile)
        return jax.shard_map(
            body,
            mesh=mesh,
            in_specs=(
                P("pole", None, "col", "row"),
                P("pole", None, "row", "col"),
                P(),
                P("pole", None),
            ),
            out_specs=(P("pole", None, "col", "row"), P(("col", "pole"), "row")),
            check_vma=False,
        )(inverse, lower, mask_tiles, pole_weight)

    return whole
```

```python
import functools

import jax
import jax.numpy as jnp
import numpy as np
from jax import lax
from jax.experimental import pallas as pl
from jax.experimental.pallas import tpu as pltpu
from jax.sharding import PartitionSpec as P

ANY = pl.BlockSpec(memory_space=pl.ANY)
SMEM = pl.BlockSpec(memory_space=pltpu.SMEM)
LANES = 128
FULL, SINGLE = 2, 1


def complex_product(block, factors):
    real_part = jnp.einsum(
        "prc,pcw->prw", block[:, 0], factors[:, 0], preferred_element_type=jnp.float32
    ) - jnp.einsum("prc,pcw->prw", block[:, 1], factors[:, 1], preferred_element_type=jnp.float32)
    imag_part = jnp.einsum(
        "prc,pcw->prw", block[:, 0], factors[:, 1], preferred_element_type=jnp.float32
    ) + jnp.einsum("prc,pcw->prw", block[:, 1], factors[:, 0], preferred_element_type=jnp.float32)
    return jnp.stack([real_part, imag_part], axis=1)


def general_body(tile, inverse, lower, mask_tiles, pole_weight):
    full_lower = lax.all_gather(lower, "col", axis=3, tiled=True)
    row_tiles = inverse.shape[2] // tile
    col_tiles = inverse.shape[3] // tile
    start = (lax.axis_index("col") * row_tiles, lax.axis_index("row") * col_tiles)
    own = lax.dynamic_slice(mask_tiles, start, (row_tiles, col_tiles))
    keep = jnp.repeat(jnp.repeat(own, tile, axis=0), tile, axis=1).astype(inverse.dtype)
    partial_value = complex_product(inverse * keep[None, None], full_lower)
    summed = lax.psum_scatter(
        partial_value.astype(jnp.bfloat16), "row", scatter_dimension=3, tiled=True
    ).astype(jnp.float32)
    panel = (-summed).astype(jnp.bfloat16)
    values = panel.astype(jnp.float32)
    weighted = jnp.sum(
        pole_weight[:, 0, None, None] * values[:, 1] + pole_weight[:, 1, None, None] * values[:, 0],
        axis=0,
    )
    density = lax.psum_scatter(
        weighted.astype(jnp.bfloat16), "pole", scatter_dimension=0, tiled=True
    ).astype(jnp.float32)
    return (panel, density)


def slice_kernel(cfg, *refs):
    pole, tile, row_tiles, n_pole = (cfg[k] for k in ("pole", "tile", "row_tiles", "n_pole"))
    parts = cfg["parts"]
    n_parts = len(parts)
    keep, fold, last = cfg["kind"] == "keep", cfg["kind"] == "fold", cfg["last"]
    low_tile, n_tiles = cfg["span"]
    folded = low_tile > 0
    span = pl.ds(low_tile * tile, n_tiles * tile)
    refs = list(refs)

    def take(count):
        taken = refs[:count]
        del refs[:count]
        return taken

    meta, weight, inv = take(3)
    cands = dict(zip(cfg["arrays"], take(len(cfg["arrays"]))))
    if keep:
        recv = take(n_parts)
        earlier = take(2 if folded else 0)
        take(cfg["aliased"])
    if fold:
        (panel,) = take(1)
    outs = take(2 if fold else 1 if keep else n_parts)
    if keep:
        (panel,) = outs
    dens = take(n_pole if last else 0)
    abuf, wbuf, prod, obuf, asem, wsem, osem = take(7)
    width = wbuf.shape[1] // (2 * n_parts)
    depth = wbuf.shape[0]
    n_buf = abuf.shape[0]

    def start(copy):
        copy.start()

    def wait(copy):
        copy.wait()

    def tile_rows(r):
        return pl.ds(pl.multiple_of(r * tile, tile), tile)

    def single(r):
        at = meta[row_tiles + r]
        return (meta[r] == SINGLE) & (at >= low_tile) & (at < low_tile + n_tiles)

    def fetch(r, act):
        slot = lax.rem(r, n_buf)

        @pl.when(meta[r] == FULL)
        def _():
            for c in range(2):
                act(pltpu.make_async_copy(inv.at[pole, c, tile_rows(r), span], abuf.at[slot, c], asem.at[slot, c]))

        @pl.when(single(r))
        def _():
            cols = tile_rows(meta[row_tiles + r])
            for c in range(2):
                act(
                    pltpu.make_async_copy(
                        inv.at[pole, c, tile_rows(r), cols], abuf.at[slot, c, :, pl.ds(0, tile)], asem.at[slot, c]
                    )
                )

    def lower_copies(j, ref):
        return [
            pltpu.make_async_copy(ref[h], wbuf.at[:, pl.ds((2 * j + h) * width, width)], wsem.at[j, h])
            for h in range(2)
        ]

    def source(name):
        whole = cands[name].at[pole] if name == "own" else cands[name]
        return [whole.at[h] if name in cfg["cut"] else whole.at[h, span, :] for h in range(2)]

    for j, (names, base) in enumerate(parts):
        for i, name in enumerate(names):

            @pl.when(meta[base] == i)
            def _(j=j, name=name):
                for copy in lower_copies(j, source(name)):
                    copy.start()

    fetch(0, start)
    columns = [pl.ds(pl.multiple_of(meta[base + 1] * width, width), width) for _, base in parts]
    extras = []
    if keep:
        rbuf, rsem = take(2)
        extras += [pltpu.make_async_copy(recv[j], rbuf.at[j], rsem.at[j]) for j in range(n_parts)]
    if fold or (last and not folded):
        pbuf, psem = take(2)
        extras += [
            pltpu.make_async_copy(panel.at[q, :, :, columns[0]], pbuf.at[q], psem.at[q]) for q in range(pole)
        ]
    if last and folded:
        held, hsem = take(2)
        base, bsem = take(2)
        extras += [pltpu.make_async_copy(earlier[0], held, hsem), pltpu.make_async_copy(earlier[1], base, bsem)]
    if last:
        d32, d16, dsem = take(3)
    for copy in extras:
        copy.start()
    for r in range(1, min(n_buf, row_tiles)):
        fetch(r, start)
    for j, (names, _) in enumerate(parts):
        for copy in lower_copies(j, source(names[0])):
            copy.wait()

    def out_copy(r, j):
        rows = tile_rows(r)
        target = panel.at[pole, :, rows, columns[j]] if keep else outs[j].at[:, rows, :]
        return pltpu.make_async_copy(obuf.at[j, :, rows, :], target, osem.at[r, j])

    def sum_copy(r):
        return pltpu.make_async_copy(sbuf.at[tile_rows(r), :], outs[1].at[tile_rows(r), :], ssem.at[r])

    def other_poles(rows):
        return sum(
            weight[q, 0] * pbuf[q, 1, rows, :].astype(jnp.float32)
            + weight[q, 1] * pbuf[q, 0, rows, :].astype(jnp.float32)
            for q in range(pole)
        )

    if fold:
        sbuf, ssem = take(2)

    def step(r, carry):
        slot = lax.rem(r, n_buf)
        rows = tile_rows(r)
        fetch(r, wait)

        @pl.when(meta[r] == FULL)
        def _():
            both = abuf[slot].reshape(2 * tile, n_tiles * tile)
            prod[...] = jnp.dot(both, wbuf[...], preferred_element_type=jnp.float32)

        @pl.when(single(r))
        def _():
            both = abuf[slot, :, :, :tile].reshape(2 * tile, tile)
            prod[...] = jnp.dot(both, wbuf[tile_rows(meta[row_tiles + r] - low_tile), :], preferred_element_type=jnp.float32)

        @pl.when((meta[r] != FULL) & jnp.logical_not(single(r)))
        def _():
            prod[...] = jnp.zeros_like(prod)

        if extras:

            @pl.when(r == 0)
            def _():
                for copy in extras:
                    copy.wait()

        if row_tiles > n_buf:

            @pl.when(r + n_buf < row_tiles)
            def _():
                fetch(r + n_buf, start)

        for j in range(n_parts):
            low, high = (pl.ds((2 * j + h) * width, width) for h in range(2))
            re = prod[:tile, low] - prod[tile:, high]
            im = prod[:tile, high] + prod[tile:, low]
            if keep:
                re = re + rbuf[j, 0, rows, :].astype(jnp.float32)
                im = im + rbuf[j, 1, rows, :].astype(jnp.float32)
                if folded:
                    re = re + held[0, rows, :]
                    im = im + held[1, rows, :]
                re, im = -re, -im
            re = re.astype(obuf.dtype)
            im = im.astype(obuf.dtype)
            obuf[j, 0, rows, :] = re
            obuf[j, 1, rows, :] = im
            out_copy(r, j).start()
        if last:
            total = weight[pole, 0] * im.astype(jnp.float32) + weight[pole, 1] * re.astype(jnp.float32)
            total = total + (base[rows, :] if folded else other_poles(rows))
            d32[rows, :] = total
            d16[rows, :] = total.astype(jnp.bfloat16)
        if fold:
            sbuf[rows, :] = other_poles(rows)
            sum_copy(r).start()
        return carry

    lax.fori_loop(0, row_tiles, step, 0)

    if last:
        share = d32.shape[0] // n_pole
        mine = meta[2 * row_tiles]
        copies = []
        for d in range(n_pole):
            block = lax.rem(mine + d, n_pole)
            rows = pl.ds(pl.multiple_of(block * share, share), share)
            copies.append(
                pltpu.make_async_copy((d16 if d else d32).at[rows, :], dens[d], dsem.at[d])
            )
        for copy in copies:
            copy.start()
        for copy in copies:
            copy.wait()

    def drain(r, carry):
        for j in range(n_parts):
            out_copy(r, j).wait()
        if fold:
            sum_copy(r).wait()
        return carry

    lax.fori_loop(0, row_tiles, drain, 0)


def slice_product(cfg, meta, weight, inverse, arrays, width, recv=None, panel=None, earlier=()):
    poles, _, rows, _ = inverse.shape
    tile, row_tiles, n_pole, parts = cfg["tile"], cfg["row_tiles"], cfg["n_pole"], cfg["parts"]
    keep, fold, last = cfg["kind"] == "keep", cfg["kind"] == "fold", cfg["last"]
    n_buf = min(row_tiles, 4)
    depth = cfg["span"][1] * tile
    n_parts = len(parts)
    names = sorted({name for part, _ in parts for name in part})
    part_shape = (2, rows, width)
    operands = [meta, weight, inverse, *(arrays[name] for name in names)]
    specs = [SMEM, SMEM] + [ANY] * (1 + len(names))
    aliases = {}
    outs = []
    if keep:
        operands += [*recv, *earlier]
        specs += [ANY] * (n_parts + len(earlier))
        outs.append(jax.ShapeDtypeStruct((poles, 2, rows, cfg["panel_width"]), jnp.bfloat16))
        if panel is not None:
            aliases = {len(operands): 0}
            operands.append(panel)
            specs.append(ANY)
    elif fold:
        operands.append(panel)
        specs.append(ANY)
        outs += [jax.ShapeDtypeStruct(part_shape, jnp.float32), jax.ShapeDtypeStruct((rows, width), jnp.float32)]
    else:
        outs += [jax.ShapeDtypeStruct(part_shape, jnp.bfloat16)] * n_parts
    if last:
        share = rows // n_pole
        for d in range(n_pole):
            outs.append(jax.ShapeDtypeStruct((share, width), jnp.bfloat16 if d else jnp.float32))
    scratch = [
        pltpu.VMEM((n_buf, 2, tile, depth), jnp.bfloat16),
        pltpu.VMEM((depth, 2 * width * n_parts), jnp.bfloat16),
        pltpu.VMEM((2 * tile, 2 * width * n_parts), jnp.float32),
        pltpu.VMEM((n_parts, *part_shape), jnp.float32 if fold else jnp.bfloat16),
        pltpu.SemaphoreType.DMA((n_buf, 2)),
        pltpu.SemaphoreType.DMA((n_parts, 2)),
        pltpu.SemaphoreType.DMA((row_tiles, n_parts)),
    ]
    if keep:
        scratch += [pltpu.VMEM((n_parts, *part_shape), jnp.bfloat16), pltpu.SemaphoreType.DMA((n_parts,))]
    if fold or (last and not earlier):
        scratch += [
            pltpu.VMEM((max(poles - 1, 1), *part_shape), jnp.bfloat16),
            pltpu.SemaphoreType.DMA((max(poles - 1, 1),)),
        ]
    if last and earlier:
        scratch += [pltpu.VMEM(part_shape, jnp.float32), pltpu.SemaphoreType.DMA]
        scratch += [pltpu.VMEM((rows, width), jnp.float32), pltpu.SemaphoreType.DMA]
    if last:
        scratch += [
            pltpu.VMEM((rows, width), jnp.float32),
            pltpu.VMEM((rows, width), jnp.bfloat16),
            pltpu.SemaphoreType.DMA((n_pole,)),
        ]
    if fold:
        scratch += [pltpu.VMEM((rows, width), jnp.float32), pltpu.SemaphoreType.DMA((row_tiles,))]
    cfg = dict(cfg, aliased=len(aliases), arrays=names)
    return pl.pallas_call(
        functools.partial(slice_kernel, cfg),
        out_shape=outs,
        in_specs=specs,
        out_specs=[ANY] * len(outs),
        scratch_shapes=scratch,
        input_output_aliases=aliases,
        compiler_params=pltpu.CompilerParams(vmem_limit_bytes=48 * 2**20),
        cost_estimate=pl.CostEstimate(flops=30 * rows * depth * n_parts, bytes_accessed=rows * width, transcendentals=0),
        name=cfg["name"],
    )(*operands)


def half_order(n_col, half, z):
    group = n_col // 2
    return sorted(range(half * group, (half + 1) * group), key=lambda s: abs(s - z))


def plan_transfers(n_col, poles):
    end, half = poles - 1, n_col // 2
    where = {(z, y, p, z): ("own", p) for z in range(n_col) for y in range(2) for p in range(poles)}
    lists = {"out": [], "across": [], "in": []}
    at = {}

    def add(kind, name, moves):
        moves = [m for m in moves if m[3] < n_col and m[4] < n_col]
        if not moves:
            return
        both = moves + [
            (n_col - 1 - z, n_col - 1 - to, p, n_col - 1 - s1, n_col - 1 - s0) for z, to, p, s0, s1 in moves
        ]
        for z, to, p, s0, s1 in both:
            where[(to, 0, p, s0)] = where[(to, 1, p, s1)] = name
        at[name] = len(lists[kind])
        lists[kind].append((name, both))

    def hop(z, p, step):
        return (z, z - 1, p, z + step - 1, z + step - 1)

    steps = range(1, n_col)
    pairs = [(p, step) for p in range(end) for step in steps]
    pairs = sorted(pairs, key=lambda item: (item[0] * (n_col - 1) + item[1] - 3 * (item[1] == 1), item))

    def add_end(i):
        far = [hop(z, end, i + 1) for z in range(2, half)]
        add("out", f"o{end}s{i + 1}", [(1, 0, end, first_row[i], second_row[i])] + [m for m in far if m[3] < n_col])

    first_row = sorted(steps, key=lambda s: (s < half, s))
    second_row = sorted(steps, key=lambda s: (s != half, s))
    def add_out(p, step):
        moves = [hop(z, p, step) for z in range(1, half)]
        inwards = [hop(z, p, step) for z in range(half + 1, n_col)]
        if step == 1 and half == 2:
            moves += inwards
            joined.add(p)
        add("out", f"o{p}s{step}", moves)

    joined = set()
    for p, step in pairs[:-1]:
        add_out(p, step)
    add_end(0)
    for p, step in pairs[-1:]:
        add_out(p, step)
    for i in range(1, len(first_row)):
        add_end(i)
    pairs = [(p, step) for p in range(poles) for step in range(1, half + 1)]
    pairs = sorted(pairs, key=lambda item: (item[0] - (item == (end, 1)), item == (end - 1, half), item))
    for p, step in pairs:
        add("across", f"a{p}s{step}", [hop(half, p, step)])
    for p in range(poles):
        for step in steps:
            if step > 1 or p not in joined:
                add("in", f"i{p}s{step}", [hop(z, p, step) for z in range(half + 1, n_col)])
    return lists, where, at


def make_fast_body(n_col, n_pole, tile):
    group = n_col // 2
    places = [(zz, yy) for zz in range(n_col) for yy in range(2)]

    def body(inverse, lower, mask_tiles, pole_weight):
        poles, _, rows, depth = inverse.shape
        width = lower.shape[3]
        row_tiles, col_tiles = rows // tile, depth // tile
        end = poles - 1
        z, y, mine = lax.axis_index("col"), lax.axis_index("row"), lax.axis_index("pole")
        lists, where, ready = plan_transfers(n_col, poles)
        final = len(lists["out"]) - 1
        final_name = lists["out"][final][0]
        cuts = col_tiles - max(1, 3 * col_tiles // 8) if col_tiles > 1 and poles > 1 else 0

        head_size = 2 * row_tiles + 1
        tables = []
        calls = []
        for p in range(poles):
            for kind in ("send", "keep"):
                for bunch in [[i] for i in range(group)]:
                    parts = []
                    for i in bunch:
                        names, picks, columns = [], np.zeros((n_col, 2), np.int32), np.zeros((n_col, 2), np.int32)
                        for zz, yy in places:
                            half = yy if kind == "keep" else 1 - yy
                            s = half_order(n_col, half, zz)[i]
                            name = where[(zz, yy, p, s)]
                            name = "own" if isinstance(name, tuple) else name
                            if name not in names:
                                names.append(name)
                            picks[zz, yy] = names.index(name)
                            columns[zz, yy] = s - half * group
                        parts.append((names, head_size + len(tables)))
                        tables += [picks, columns]
                    calls.append((p, kind, tuple(bunch), parts))
        chosen = lax.dynamic_slice(jnp.asarray(np.stack(tables)), (0, z, y), (len(tables), 1, 1)).reshape(-1)

        own = lax.dynamic_slice(mask_tiles, (z * row_tiles, y * col_tiles), (row_tiles, col_tiles))
        count = jnp.sum(own, axis=1)
        modes = jnp.where(count == col_tiles, FULL, jnp.where(count == 0, 0, SINGLE))
        single = jnp.argmax(own, axis=1)
        meta = jnp.concatenate([modes, single, jnp.reshape(mine, (1,)), chosen]).astype(jnp.int32)

        arrays = {"own": lower}
        rest = lower
        for p in range(poles):
            arrays[("own", p)] = rest[p]
            rest, arrays[("own", p)] = lax.optimization_barrier((rest, arrays[("own", p)]))

        queue = [[] for _ in range(final + 1)]
        sent_at = {}
        for call in calls:
            p, kind, bunch, parts = call
            t = max([ready.get(name, 0) for names, _ in parts for name in names])
            if kind == "send":
                sent_at.update({(p, i): t for i in bunch})
            else:
                t = min(max([t] + [sent_at[(p, i)] + 1 for i in bunch]), final)
            queue[t].append(call)

        late = {"meta": meta}
        state = {"panel": None, "part": {}, "sent": {}, "dens": {}}

        def run(call):
            p, kind, bunch, parts = call
            cfg = dict(
                name=f"{kind}_{p}_{bunch[0]}",
                kind=kind,
                last=kind == "keep" and p == end,
                parts=parts,
                pole=p,
                tile=tile,
                row_tiles=row_tiles,
                n_pole=n_pole,
                panel_width=group * width,
                span=(0, col_tiles),
                cut=[],
            )
            if kind == "send":
                made = slice_product(cfg, late["meta"], pole_weight, inverse, arrays, width)
                for i, part in zip(bunch, made):
                    state["part"][(p, i)] = part
                    state["sent"][(p, i)] = lax.ppermute(part, "row", [(0, 1), (1, 0)])
                return
            recv = [state["sent"][(p, i)] for i in bunch]
            sources, earlier = arrays, ()
            if cuts and final_name in parts[0][0]:
                sources = dict(arrays, **{final_name: arrays[final_name][0]})
                first = dict(cfg, name=f"fold_{p}_{bunch[0]}", kind="fold", last=False, span=(0, cuts), cut=[final_name])
                earlier = slice_product(
                    first, late["meta"], pole_weight, inverse, sources, width, panel=state["panel"]
                )
                sources = dict(arrays, **{final_name: arrays[final_name][1]})
                cfg.update(span=(cuts, col_tiles - cuts), cut=[final_name])
            panel, *shares = slice_product(
                cfg, late["meta"], pole_weight, inverse, sources, width, recv, state["panel"], earlier
            )
            state["panel"] = panel
            if shares:
                total = shares[0]
                for d in range(1, n_pole):
                    ways = [(q, (q + d) % n_pole) for q in range(n_pole)]
                    total = total + lax.ppermute(shares[d], "pole", ways).astype(jnp.float32)
                state["dens"][bunch[0]] = total

        def is_one_of(spots):
            return functools.reduce(jnp.logical_or, [(z == a) & (y == b) for a, b in spots])

        def launch(kind, t, deps):
            if t >= len(lists[kind]):
                return
            name, moves = lists[kind][t]
            held = {}
            for zz, _, p, s0, s1 in moves:
                for yy, s in ((0, s0), (1, s1)):
                    held.setdefault(where[(zz, yy, p, s)], []).append((zz, yy))
            held = sorted(held.items(), key=lambda item: -len(item[1]))
            values = [arrays[source] for source, _ in held]
            values, state["panel"], _ = lax.optimization_barrier((values, state["panel"], deps))
            ways = [(zz, to) for zz, to, *_ in moves]
            pieces = [slice(None)]
            if name == final_name and cuts:
                pieces = [slice(0, cuts * tile), slice(cuts * tile, None)]
            moved = []
            for piece in pieces:
                value = values[0][:, piece]
                for other, (_, spots) in zip(values[1:], held[1:]):
                    value = jnp.where(is_one_of(spots), other[:, piece], value)
                moved.append(value)
            moved = [lax.ppermute(value, "col", ways) for value in lax.optimization_barrier(moved)]
            arrays[name] = moved if len(moved) > 1 else moved[0]

        def landed(kind, t):
            return [arrays[lists[kind][t][0]]] if 0 <= t < len(lists[kind]) else []

        launch("out", 0, [])
        launch("across", 0, [])
        launch("out", 1, [])
        launch("across", 1, [])
        for t in range(final + 1):
            deps = landed("out", t)
            deps += [state["part"][key] for key, at in sent_at.items() if at == t - 1]
            deps += [state["sent"][key] for key, at in sent_at.items() if at == t - 2]
            launch("out", t + 2, deps)
            launch("across", t + 2, landed("out", t) + landed("across", t))
            launch("in", t, landed("out", t) + landed("in", t - 1))
            for kind in ("send", "keep"):
                for call in queue[t]:
                    if call[1] == kind:
                        run(call)
                if t >= final - 2:
                    made = [state["part"][key] for key, at in sent_at.items() if at == t]
                    late["meta"], state["panel"], _ = lax.optimization_barrier((late["meta"], state["panel"], made))

        columns = []
        for c in range(group):
            value = state["dens"][0]
            for i in range(1, group):
                spots = [(a, b) for a, b in places if half_order(n_col, b, a)[i] - b * group == c]
                value = jnp.where(is_one_of(spots), state["dens"][i], value)
            columns.append(value)
        return (state["panel"], jnp.concatenate(columns, axis=1))

    return body


def solution(mesh):
    n_pole, n_row, n_col = (mesh.shape[name] for name in ("pole", "row", "col"))

    def whole(inverse, lower, mask_tiles, pole_weight):
        tile = inverse.shape[2] // mask_tiles.shape[0]
        width = lower.shape[3] // n_col
        rows = inverse.shape[2] // n_col
        fits = n_row == 2 and n_col % 2 == 0 and n_col > 2 and width % LANES == 0
        fits = fits and tile % LANES == 0 and rows % (16 * n_pole) == 0 and inverse.shape[0] > n_pole
        if fits:
            body = make_fast_body(n_col, n_pole, tile)
        else:
            body = functools.partial(general_body, tile)
        return jax.shard_map(
            body,
            mesh=mesh,
            in_specs=(
                P("pole", None, "col", "row"),
                P("pole", None, "row", "col"),
                P(),
                P("pole", None),
            ),
            out_specs=(P("pole", None, "col", "row"), P(("col", "pole"), "row")),
            check_vma=False,
        )(inverse, lower, mask_tiles, pole_weight)

    return whole
```
